128 devices in a mesh: row: 8 (over z_lo, x), col: 16 (over y, z_hi, core).
Axes of the slice: x: 4, y: 4, z: 4 (z_hi: 2, z_lo: 2; z = z_hi * 2 + z_lo), core: 2. Of those that a mesh axis runs over, the one named last changes fastest.
Arguments:
- tokens: bfloat16 [512, 512, 384], P('row', 'col'), may hold values from -25 to 25
- tissue: int32 [512, 512], P('row', 'col'), may hold values from 0 to 1, as said below
- cotangent: bfloat16 [512, 512, 384], P('row', 'col'), may hold values from -6 to 6
- packed_weight: bfloat16 [384, 1152], replicated, may hold values from -0.3125 to 0.3125
- output_weight: bfloat16 [384, 384], replicated, may hold values from -0.3125 to 0.3125
Outputs:
- layer_out: bfloat16 [512, 512, 384], P('row', 'col')
- grad_tokens: bfloat16 [512, 512, 384], P('row', 'col')
- grad_packed: float32 [384, 1152], replicated
- grad_output: float32 [384, 384], replicated
The draws below stay inside these ranges and needn't reach their ends.
Inputs may be any that keep to these rules, and one draw needn't show every extreme that they name: 1 marks a tissue token, 0 background.
All inputs are finite; a program needn't handle non-finite values.
Results may differ from the reference program's by a relative error of at most 0.004.
The reference program's roundings to bfloat16 on the way count: a program that leaves them out, or rounds other values in their place, can miss the bound.
Values may be sent and summed in bfloat16 or wider, within the bound.
No kernel may reach another device: no remote copies, remote signals or barrier semaphores. Data moves between devices by JAX's collectives and lax.ppermute only.
A program may use at most 128 MiB of HBM per device.

```python
import jax
import jax.numpy as jnp
from jax import lax

D = 384
HEADS = 6
HEAD = 64
KERNEL = 7
RADIUS = 3
NR = 512
NC = 512
TOKENS = 262144


def draw_tokens(key, part):
    key = jax.random.fold_in(key, 5)
    normal_key = jax.random.fold_in(key, 0)
    normal_part = jnp.clip(jax.random.normal(normal_key, (NR, NC, D), jnp.float32), -5.0, 5.0)
    return normal_part.astype(jnp.bfloat16)


def draw_tissue(key, part):
    key = jax.random.fold_in(key, 11)
    coarse_key, fine_key = jax.random.split(key)
    coarse = jax.random.randint(coarse_key, ((NR + 31) // 32, (NC + 31) // 32), 0, 5)
    region_level = jnp.repeat(jnp.repeat(coarse, 32, axis=0), 32, axis=1)[:NR, :NC]
    fine_draw = jax.random.randint(fine_key, (NR, NC), 0, 4)
    return (fine_draw < region_level).astype(jnp.int32)


def block_levels(key, shape, cuts, least, high):
    gain, own = 1.0, jax.random.fold_in(key, 6)
    for dim, shards_of in cuts:
        draws = jnp.exp(jax.random.uniform(jax.random.fold_in(own, dim), (shards_of,), jnp.float32, least / len(cuts), high / len(cuts)))
        gain = gain * jnp.repeat(draws, shape[dim] // shards_of).reshape([-1 if axis == dim else 1 for axis in range(len(shape))])
    return gain


def normal_values(key, extent, deviation, bound, pieces=(), kind=jnp.bfloat16):
    values = jax.random.normal(key, extent, jnp.float32) * deviation
    if len(pieces) > 0:
        values = block_levels(key, extent, pieces, -0.22, 0.18) * values
    return jnp.clip(values, min=-bound, max=bound).astype(kind)


def setup_inputs(seed: int = 0) -> dict:
    seeds = jax.random.split(jax.random.key(seed), 6)
    return {
        "tokens": draw_tokens(jax.random.fold_in(seeds[5], 71), 0),
        "tissue": draw_tissue(jax.random.fold_in(seeds[5], 71), 0),
        "cotangent": normal_values(seeds[2], (NR, NC, D), 1.0, 6.0, ((0, 8), (1, 16))),
        "packed_weight": normal_values(seeds[3], (D, 3 * D), D ** -0.5, 0.3125),
        "output_weight": normal_values(seeds[4], (D, D), D ** -0.5, 0.3125),
    }


def reference(tokens, tissue, cotangent, packed_weight, output_weight):
    factor = HEAD ** -0.5
    grad_scale = TOKENS ** -0.5
    token_rows = tokens.reshape(-1, D)
    packed = jnp.dot(token_rows, packed_weight, preferred_element_type=jnp.float32).astype(jnp.bfloat16).reshape(NR, NC, 3 * D)
    query_part = packed[..., :D].reshape(NR, NC, HEADS, HEAD).astype(jnp.float32)
    key_part = packed[..., D:2 * D]
    value_part = packed[..., 2 * D:]
    row_ids = jnp.arange(NR, dtype=jnp.int32)
    col_ids = jnp.arange(NC, dtype=jnp.int32)
    row_start = jnp.clip(row_ids - RADIUS, 0, NR - KERNEL).astype(jnp.int32)
    col_start = jnp.clip(col_ids - RADIUS, 0, NC - KERNEL).astype(jnp.int32)
    tissue_keys = tissue == 1
    offsets = jnp.arange(KERNEL * KERNEL, dtype=jnp.int32)

    def places(offset):
        row_pick = (row_start + offset // KERNEL).astype(jnp.int32)
        col_pick = (col_start + offset % KERNEL).astype(jnp.int32)
        return row_pick, col_pick

    def nearby(array, offset):
        row_pick, col_pick = places(offset)
        return jnp.take(jnp.take(array, row_pick, axis=0), col_pick, axis=1)

    def split_heads(array):
        return array.reshape(NR, NC, HEADS, HEAD).astype(jnp.float32)

    def score_at(offset):
        row_pick, col_pick = places(offset)
        scores = jnp.sum(query_part * split_heads(nearby(key_part, offset)), axis=-1) * factor
        own_key = (row_pick[:, None] == row_ids[:, None]) & (col_pick == col_ids)[None, :]
        keep_key = nearby(tissue_keys, offset) | own_key
        return scores, keep_key

    scores, keep_key = lax.map(score_at, offsets)
    masked = jnp.where(keep_key[..., None], scores, -jnp.inf)
    row_top = jnp.max(masked, axis=0)
    exp_terms = jnp.where(keep_key[..., None], jnp.exp(masked - row_top), 0.0)
    prob_full = exp_terms / jnp.sum(exp_terms, axis=0)
    prob_low = prob_full.astype(jnp.bfloat16)

    def mix_step(running, offset):
        weight_now = prob_low[offset].astype(jnp.float32)[..., None]
        return running + weight_now * split_heads(nearby(value_part, offset)), None

    mixture, _ = lax.scan(mix_step, jnp.zeros((NR, NC, HEADS, HEAD), jnp.float32), offsets)
    tissue_float = tissue.astype(jnp.float32)[..., None]
    attended = (tissue_float * mixture.reshape(NR, NC, D)).astype(jnp.bfloat16)
    attended_rows = attended.reshape(-1, D)
    layer_out = (token_rows.astype(jnp.float32) + jnp.dot(attended_rows, output_weight, preferred_element_type=jnp.float32)).astype(jnp.bfloat16).reshape(NR, NC, D)

    cotangent_rows = cotangent.reshape(-1, D)
    grad_att = (tissue_float.reshape(-1, 1) * jnp.dot(cotangent_rows, output_weight.T, preferred_element_type=jnp.float32)).astype(jnp.bfloat16)
    grad_heads = split_heads(grad_att.reshape(NR, NC, D))

    def slopes_at(offset):
        return jnp.sum(grad_heads * split_heads(nearby(value_part, offset)), axis=-1)

    prob_slope = lax.map(slopes_at, offsets)
    prob_delta = jnp.sum(prob_full * prob_slope, axis=0)
    score_grad = (prob_full * (prob_slope - prob_delta) * factor).astype(jnp.bfloat16)

    def back_step(carry, offset):
        query_grad, pair_grad = carry
        row_pick, col_pick = places(offset)
        slope_weight = score_grad[offset].astype(jnp.float32)[..., None]
        query_grad = query_grad + slope_weight * split_heads(nearby(key_part, offset))
        key_piece = (slope_weight * query_part).reshape(NR, NC, D)
        value_piece = (prob_low[offset].astype(jnp.float32)[..., None] * grad_heads).reshape(NR, NC, D)
        grad_piece = jnp.concatenate([key_piece, value_piece], axis=-1)
        pair_grad = pair_grad.at[row_pick[:, None], col_pick[None, :]].add(grad_piece)
        return (query_grad, pair_grad), None

    start_carry = (jnp.zeros((NR, NC, HEADS, HEAD), jnp.float32), jnp.zeros((NR, NC, 2 * D), jnp.float32))
    (query_grad, pair_grad), _ = lax.scan(back_step, start_carry, offsets)
    packed_grad = jnp.concatenate([query_grad.reshape(NR, NC, D), pair_grad], axis=-1).reshape(-1, 3 * D).astype(jnp.bfloat16)
    grad_tokens = (cotangent_rows.astype(jnp.float32) + jnp.dot(packed_grad, packed_weight.T, preferred_element_type=jnp.float32)).astype(jnp.bfloat16).reshape(NR, NC, D)
    grad_packed = jnp.dot(token_rows.T, packed_grad, preferred_element_type=jnp.float32) * grad_scale
    grad_output = jnp.dot(attended_rows.T, cotangent_rows, preferred_element_type=jnp.float32) * grad_scale
    return layer_out, grad_tokens, grad_packed, grad_output
```

```python
import functools

import jax
import jax.numpy as jnp
from jax import lax
from jax.experimental import pallas as pl
from jax.experimental.pallas import tpu as pltpu
from jax.sharding import PartitionSpec as P

HEADS = 6
HEAD = 64
KERNEL = 7
RADIUS = 3
PAIR = 2 * HEAD
PAIRS = HEADS // 2
SIDE = 8
TILE_ROWS = 4
FACTOR = HEAD ** (-0.5)
NEG = float("-inf")
f32 = jnp.float32
bf16 = jnp.bfloat16


def dims(lhs, rhs):
    return (((lhs,), (rhs,)), ((), ()))


def attention_kernel(
    own_ref, side_ref, cot_ref, wp_ref, wo_ref, tis_own_ref, tis_side_ref, win_ref, self_ref, gate_ref,
    att_ref, dq_ref, dkv_own_ref, dkv_side_ref,
    q_s, g_s, kv_own_s, kv_side_s,
):
    rows_own, width = own_ref.shape
    rows_side = side_ref.shape[0]
    tokens_dev = cot_ref.shape[0]
    cols = (rows_own - tokens_dev) // (2 * RADIUS)
    halo = RADIUS * cols
    tile = TILE_ROWS * cols
    tiles = tokens_dev // tile
    own_keys = (TILE_ROWS + 2 * RADIUS) * cols
    side_keys = (TILE_ROWS + 2 * RADIUS) * SIDE

    kv_own_s[...] = jnp.dot(
        own_ref[...], wp_ref[:, width:], preferred_element_type=f32
    ).astype(bf16)
    kv_side_s[...] = jnp.dot(
        side_ref[...], wp_ref[:, width:], preferred_element_type=f32
    ).astype(bf16)
    q_s[...] = (
        jnp.dot(
            own_ref[halo : halo + tokens_dev, :], wp_ref[:, :width], preferred_element_type=f32
        ).astype(bf16)
        * FACTOR
    ).astype(bf16)
    g_s[...] = lax.dot_general(
        cot_ref[...], wo_ref[...], dims(1, 1), preferred_element_type=f32
    ).astype(bf16)
    dkv_own_ref[...] = jnp.zeros_like(dkv_own_ref)
    dkv_side_ref[...] = jnp.zeros_like(dkv_side_ref)

    first_head = lax.broadcasted_iota(jnp.int32, (tile, PAIR), 1) < HEAD

    def split(block):
        zero = jnp.zeros_like(block)
        return jnp.concatenate(
            [jnp.where(first_head, block, zero), jnp.where(first_head, zero, block)], axis=0
        )

    def joined(both):
        return jnp.concatenate([both[:HEAD, :tile], both[HEAD:, tile:]], axis=0).T

    def step(index, carry):
        q_at = pl.ds(pl.multiple_of(index * tile, tile), tile)
        own_at = pl.ds(pl.multiple_of(index * tile, tile), own_keys)
        side_at = pl.ds(pl.multiple_of(index * TILE_ROWS * SIDE, TILE_ROWS * SIDE), side_keys)
        kind = jnp.where(index == 0, 0, jnp.where(index == tiles - 1, 2, 1))
        tis_keys = jnp.concatenate([tis_own_ref[own_at, :], tis_side_ref[side_at, :]], axis=0)
        bias = jnp.maximum(tis_keys, self_ref[...]) + win_ref[kind]
        bias = jnp.concatenate([bias, bias], axis=1)
        gate = gate_ref[index]
        for pair in range(PAIRS):
            at = slice(pair * PAIR, (pair + 1) * PAIR)
            v_at = slice(width + pair * PAIR, width + (pair + 1) * PAIR)
            keys = jnp.concatenate([kv_own_s[own_at, at], kv_side_s[side_at, at]], axis=0)
            values = jnp.concatenate([kv_own_s[own_at, v_at], kv_side_s[side_at, v_at]], axis=0)
            query = split(q_s[q_at, at])
            grad = split(g_s[q_at, at])
            scores = lax.dot_general(keys, query, dims(1, 1), preferred_element_type=f32) + bias
            top = jnp.max(scores, axis=0, keepdims=True)
            terms = jnp.exp(scores - top)
            total = jnp.sum(terms, axis=0, keepdims=True)
            slope = lax.dot_general(values, grad, dims(1, 1), preferred_element_type=f32)
            inverse = 1.0 / total
            delta = jnp.sum(terms * slope, axis=0, keepdims=True) * inverse
            probs = terms * (inverse * gate)
            probs_low = probs.astype(bf16)
            score_grad = (probs * (slope - delta)).astype(bf16)
            mix = lax.dot_general(values, probs_low, dims(0, 0), preferred_element_type=f32)
            att_ref[q_at, at] = joined(mix).astype(bf16)
            dq = lax.dot_general(keys, score_grad, dims(0, 0), preferred_element_type=f32)
            dq_ref[q_at, at] = (joined(dq) * FACTOR).astype(bf16)
            dk = jnp.dot(score_grad, query, preferred_element_type=f32)
            dv = jnp.dot(probs_low, grad, preferred_element_type=f32)
            dkv_own_ref[own_at, at] += dk[:own_keys]
            dkv_side_ref[side_at, at] += dk[own_keys:]
            dkv_own_ref[own_at, v_at] += dv[:own_keys]
            dkv_side_ref[side_at, v_at] += dv[own_keys:]
        return carry

    lax.fori_loop(0, tiles, step, 0)


def attention(own, side, cot, wp, wo, tis_own, tis_side, win, self_bias, gate):
    tokens_dev, width = cot.shape
    vmem = pl.BlockSpec(memory_space=pltpu.VMEM)
    return pl.pallas_call(
        attention_kernel,
        out_shape=[
            jax.ShapeDtypeStruct((tokens_dev, width), bf16),
            jax.ShapeDtypeStruct((tokens_dev, width), bf16),
            jax.ShapeDtypeStruct((own.shape[0], 2 * width), f32),
            jax.ShapeDtypeStruct((side.shape[0], 2 * width), f32),
        ],
        in_specs=[vmem] * 10,
        out_specs=[vmem] * 4,
        scratch_shapes=[
            pltpu.VMEM((tokens_dev, width), bf16),
            pltpu.VMEM((tokens_dev, width), bf16),
            pltpu.VMEM((own.shape[0], 2 * width), bf16),
            pltpu.VMEM((side.shape[0], 2 * width), bf16),
        ],
        compiler_params=pltpu.CompilerParams(vmem_limit_bytes=56 * 1024 * 1024),
        name="attention",
    )(own, side, cot, wp, wo, tis_own, tis_side, win, self_bias, gate)


def to_next(array, axis):
    count = lax.axis_size(axis)
    return lax.ppermute(array, axis, [(i, (i + 1) % count) for i in range(count)])


def to_last(array, axis):
    count = lax.axis_size(axis)
    return lax.ppermute(array, axis, [((i + 1) % count, i) for i in range(count)])


def total_over_devices(partial):
    axes = ("row", "col")
    count = lax.axis_size("row") * lax.axis_size("col")
    rows, cols = partial.shape
    pieces = partial.astype(bf16).reshape(count, rows * cols // count // 128, 128)
    pieces = lax.all_to_all(pieces, axes, 0, 0, tiled=True)
    mine = jnp.sum(pieces.astype(f32), axis=0).astype(bf16)
    copies = jnp.broadcast_to(mine[None], (count,) + mine.shape)
    whole = lax.all_to_all(copies, axes, 0, 0, tiled=True)
    return whole.astype(f32).reshape(rows, cols)


def mask_parts(rows_dev, cols_dev):
    row_base = lax.axis_index("row") * rows_dev
    col_base = lax.axis_index("col") * cols_dev
    grid_rows = rows_dev * lax.axis_size("row")
    grid_cols = cols_dev * lax.axis_size("col")
    key_rows = TILE_ROWS + 2 * RADIUS
    far = -(2 ** 20)
    side_cols = [i - RADIUS for i in range(RADIUS)] + [cols_dev + i for i in range(RADIUS)]
    side_cols += [far] * (SIDE - len(side_cols))
    col_own = jnp.tile(jnp.arange(cols_dev, dtype=jnp.int32), key_rows)
    col_side = jnp.tile(jnp.array(side_cols, jnp.int32), key_rows)
    key_col = jnp.concatenate([col_own, col_side])
    row_ids = jnp.arange(key_rows, dtype=jnp.int32) - RADIUS
    key_row = jnp.concatenate([jnp.repeat(row_ids, cols_dev), jnp.repeat(row_ids, SIDE)])
    query_col = jnp.tile(jnp.arange(cols_dev, dtype=jnp.int32), TILE_ROWS)
    query_row = jnp.repeat(jnp.arange(TILE_ROWS, dtype=jnp.int32), cols_dev)
    same = (key_col[:, None] == query_col[None, :]) & (key_row[:, None] == query_row[None, :])
    self_bias = jnp.where(same, 0.0, NEG).astype(f32)

    def inside(key, query, base, extent):
        start = jnp.clip(base + query - RADIUS, 0, extent - KERNEL)
        offset = (base + key)[:, None] - start[None, :]
        return (offset >= 0) & (offset < KERNEL)

    col_in = inside(key_col, query_col, col_base, grid_cols)
    kinds = []
    for first in (0, 2 * TILE_ROWS, rows_dev - TILE_ROWS):
        row_in = inside(key_row, query_row, row_base + first, grid_rows)
        kinds.append(jnp.where(col_in & row_in, 0.0, NEG).astype(f32))
    return jnp.stack(kinds), self_bias


def per_device(tokens, tissue, cotangent, packed_weight, output_weight):
    rows_dev, cols_dev, width = tokens.shape
    ext_rows = rows_dev + 2 * RADIUS
    total_scale = float(rows_dev * lax.axis_size("row") * cols_dev * lax.axis_size("col")) ** (-0.5)
    token_rows = tokens.reshape(-1, width)
    cotangent_rows = cotangent.reshape(-1, width)

    with_tissue = lambda a, b: jnp.concatenate([a, b.astype(bf16)[..., None]], axis=-1)
    above = to_next(with_tissue(tokens[-RADIUS:], tissue[-RADIUS:]), "row")
    below = to_last(with_tissue(tokens[:RADIUS], tissue[:RADIUS]), "row")
    left_cols = with_tissue(tokens[:, :RADIUS], tissue[:, :RADIUS])
    right_cols = with_tissue(tokens[:, -RADIUS:], tissue[:, -RADIUS:])
    left_cols = jnp.concatenate([above[:, :RADIUS], left_cols, below[:, :RADIUS]], axis=0)
    right_cols = jnp.concatenate([above[:, -RADIUS:], right_cols, below[:, -RADIUS:]], axis=0)
    from_left = to_next(right_cols, "col")
    from_right = to_last(left_cols, "col")
    pad = jnp.zeros((ext_rows, SIDE - 2 * RADIUS, width + 1), bf16)
    side = jnp.concatenate([from_left, from_right, pad], axis=1).reshape(-1, width + 1)
    own = jnp.concatenate([above[..., :width], tokens, below[..., :width]], axis=0).reshape(
        -1, width
    )
    tis_own = jnp.concatenate([above[..., width], tissue.astype(bf16), below[..., width]], axis=0)

    def lanes(mask):
        bias = jnp.where(mask.reshape(-1, 1) > 0.5, 0.0, NEG).astype(f32)
        return jnp.broadcast_to(bias, (bias.shape[0], TILE_ROWS * cols_dev))

    win, self_bias = mask_parts(rows_dev, cols_dev)
    gate = tissue.reshape(-1, 1, TILE_ROWS * cols_dev).astype(f32)
    gate = jnp.concatenate([gate, gate], axis=2)
    side_tokens = side[:, :width]
    attended, dq, dkv_own, dkv_side = attention(
        own, side_tokens, cotangent_rows, packed_weight, output_weight,
        lanes(tis_own), lanes(side[:, width]), win, self_bias, gate,
    )

    contract = functools.partial(lax.dot_general, preferred_element_type=f32)
    output_partial = contract(attended, cotangent_rows, dims(0, 0))
    q_partial = contract(token_rows, dq, dims(0, 0))
    kv_partial = contract(own, dkv_own.astype(bf16), dims(0, 0)) + contract(
        side_tokens, dkv_side.astype(bf16), dims(0, 0)
    )
    partial = jnp.concatenate([q_partial, kv_partial, output_partial], axis=1)

    dkv_side = dkv_side.reshape(ext_rows, SIDE, 2 * width)
    dkv_own = dkv_own.reshape(ext_rows, cols_dev, 2 * width)
    to_left = to_last(dkv_side[:, :RADIUS].astype(bf16), "col")
    to_right = to_next(dkv_side[:, RADIUS : 2 * RADIUS].astype(bf16), "col")
    middle = jnp.zeros((ext_rows, cols_dev - 2 * RADIUS, 2 * width), bf16)
    dkv_own = dkv_own + jnp.concatenate([to_right, middle, to_left], axis=1).astype(f32)
    to_above = to_last(dkv_own[:RADIUS].astype(bf16), "row")
    to_below = to_next(dkv_own[-RADIUS:].astype(bf16), "row")
    middle = jnp.zeros((rows_dev - 2 * RADIUS, cols_dev, 2 * width), bf16)
    dkv = dkv_own[RADIUS:-RADIUS] + jnp.concatenate([to_below, middle, to_above], axis=0).astype(f32)
    dkv = dkv.astype(bf16).reshape(-1, 2 * width)

    layer_out = (
        token_rows.astype(f32) + jnp.dot(attended, output_weight, preferred_element_type=f32)
    ).astype(bf16)
    grad_tokens = (
        cotangent_rows.astype(f32)
        + contract(dq, packed_weight[:, :width], dims(1, 1))
        + contract(dkv, packed_weight[:, width:], dims(1, 1))
    ).astype(bf16)
    sums = total_over_devices(partial) * total_scale
    return (
        layer_out.reshape(rows_dev, cols_dev, width),
        grad_tokens.reshape(rows_dev, cols_dev, width),
        sums[:, : 3 * width],
        sums[:, 3 * width :],
    )


def solution(mesh):
    in_specs = (P("row", "col", None), P("row", "col"), P("row", "col", None), P(), P())
    out_specs = (P("row", "col", None), P("row", "col", None), P(), P())
    return jax.shard_map(
        per_device, mesh=mesh, in_specs=in_specs, out_specs=out_specs, check_vma=False
    )
```

```python
import functools

import jax
import jax.numpy as jnp
from jax import lax
from jax.experimental import pallas as pl
from jax.experimental.pallas import tpu as pltpu
from jax.sharding import PartitionSpec as P

HEADS = 6
HEAD = 64
KERNEL = 7
RADIUS = 3
PAIR = 2 * HEAD
PAIRS = HEADS // 2
SIDE = 8
TILE_ROWS = 4
KEY_ROWS = TILE_ROWS + 2 * RADIUS
CHUNK = 80
FACTOR = HEAD ** (-0.5)
NEG = float("-inf")
MIB = 1024 * 1024
f32 = jnp.float32
bf16 = jnp.bfloat16


def dims(lhs, rhs):
    return (((lhs,), (rhs,)), ((), ()))


def attention_kernel(
    extents,
    above_ref, below_ref, side_ref, tok_hbm, cot_hbm, wp_ref, wo_ref, base_ref, tissue_ref,
    att_hbm, dq_hbm, dkv_own_hbm, to_left_ref, to_right_ref, part_ref,
    tok_ref, cot_ref, q_ref, g_ref, tok_t_ref, att_ref, dq_ref, dkv_own_ref, dkv_side_ref,
    kv_own_s, kv_side_s, tis_own_s, tis_side_s, bias_s, win_ref, self_ref, att_t_s, acc_own, acc_side, sems, *stage,
):
    tokens_dev, width = q_ref.shape
    halo = above_ref.shape[0]
    rows_own = tokens_dev + 2 * halo
    cols = halo // RADIUS
    tile = TILE_ROWS * cols
    tiles = tokens_dev // tile
    own_keys = rows_own - tokens_dev + tile
    side_keys = KEY_ROWS * SIDE
    keys_all = own_keys + side_keys
    x_s, dp_s, top_s, pl_s, sg_s = (stage[i * PAIRS : (i + 1) * PAIRS] for i in range(5))

    middle = pl.ds(halo, tokens_dev)
    early = [
        pltpu.make_async_copy(tok_hbm, tok_ref, sems.at[0]),
        pltpu.make_async_copy(cot_hbm, cot_ref, sems.at[1]),
    ]
    for copy in early:
        copy.start()

    def lanes(column):
        bias = jnp.where(column.astype(f32) > 0.5, 0.0, NEG)
        return jnp.broadcast_to(bias, (bias.shape[0], tile))

    def outer(rows_ref):
        return jnp.dot(
            rows_ref[:, :width], wp_ref[:, width:], preferred_element_type=f32
        ).astype(bf16)

    kv_own_s[:halo] = outer(above_ref)
    kv_own_s[halo + tokens_dev :] = outer(below_ref)
    kv_side_s[...] = outer(side_ref)
    tis_own_s[:halo] = lanes(above_ref[:, width : width + 1])
    tis_own_s[halo + tokens_dev :] = lanes(below_ref[:, width : width + 1])
    tis_side_s[...] = lanes(side_ref[:, width : width + 1])
    lane = lax.broadcasted_iota(jnp.int32, (1, tile), 1)
    query_row = sum((lane >= i * cols).astype(jnp.int32) for i in range(1, TILE_ROWS))
    query_col = lane - query_row * cols

    def window(key, query, base, extent):
        start = jnp.clip(base + query - RADIUS, 0, extent - KERNEL) - base
        return jnp.where((key >= start) & (key < start + KERNEL), 0.0, NEG)

    own_col = lax.broadcasted_iota(jnp.int32, (cols, tile), 0)
    side_col = lax.broadcasted_iota(jnp.int32, (SIDE, tile), 0) - RADIUS
    side_col = jnp.where(side_col < 0, side_col, side_col + cols)
    side_col = jnp.where(side_col < cols + RADIUS, side_col, -(2**20))
    own_in = window(own_col, query_col, base_ref[1], extents[1])
    side_in = window(side_col, query_col, base_ref[1], extents[1])
    own_same = jnp.where(own_col == query_col, 0.0, NEG)
    for key_row in range(KEY_ROWS):
        own_rows = slice(key_row * cols, (key_row + 1) * cols)
        side_rows = slice(own_keys + key_row * SIDE, own_keys + (key_row + 1) * SIDE)
        for kind, first in enumerate((0, 2 * TILE_ROWS, (tiles - 1) * TILE_ROWS)):
            row_in = window(key_row - RADIUS, query_row, base_ref[0] + first, extents[0])
            win_ref[kind, own_rows] = own_in + row_in
            win_ref[kind, side_rows] = side_in + row_in
        row_same = jnp.where(query_row == key_row - RADIUS, 0.0, NEG)
        self_ref[own_rows] = own_same + row_same
        self_ref[side_rows] = jnp.full((SIDE, tile), NEG, f32)
    for index in range(tiles):
        across = jnp.broadcast_to(tissue_ref[index].astype(f32), (tile, tile)).T
        rows = slice(halo + index * tile, halo + (index + 1) * tile)
        tis_own_s[rows] = jnp.where(across > 0.5, 0.0, NEG)
    for copy in early:
        copy.wait()
    kv_own_s[middle] = outer(tok_ref)
    q = jnp.dot(tok_ref[...], wp_ref[:, :width], preferred_element_type=f32).astype(bf16)
    q_ref[...] = (q * FACTOR).astype(bf16)
    g_ref[...] = lax.dot_general(
        cot_ref[...], wo_ref[...], dims(1, 1), preferred_element_type=f32
    ).astype(bf16)
    tok_t_ref[...] = tok_ref[...].T
    seen_own = own_keys - tile
    seen_side = side_keys - TILE_ROWS * SIDE
    acc_own[:seen_own] = jnp.zeros((seen_own, 2 * width), f32)
    acc_side[:seen_side] = jnp.zeros((seen_side, 2 * width), f32)
    pl_s[-1][...] = jnp.zeros((keys_all, 2 * tile), bf16)
    sg_s[-1][...] = jnp.zeros((keys_all, 2 * tile), bf16)

    first_head = lax.broadcasted_iota(jnp.int32, (tile, PAIR), 1) < HEAD

    def split(block):
        zero = jnp.zeros_like(block)
        return jnp.concatenate(
            [jnp.where(first_head, block, zero), jnp.where(first_head, zero, block)], axis=0
        )

    def joined(both):
        return jnp.concatenate([both[:HEAD, :tile], both[HEAD:, tile:]], axis=0)

    def places(index, base, size, step):
        return pl.ds(pl.multiple_of(index * step, step) + base, size)

    def q_at(index):
        return places(index, 0, tile, tile)

    def own_at(index, base=0, size=own_keys):
        return places(index, base, size, tile)

    def side_at(index, base=0, size=side_keys):
        return places(index, base, size, TILE_ROWS * SIDE)

    def pair_cols(pair):
        return slice(pair * PAIR, (pair + 1) * PAIR), slice(
            width + pair * PAIR, width + (pair + 1) * PAIR
        )

    def key_rows(index, at):
        return jnp.concatenate([kv_own_s[own_at(index), at], kv_side_s[side_at(index), at]], axis=0)

    def make_bias(index):
        kind = jnp.where(index == 0, 0, jnp.where(index == tiles - 1, 2, 1))
        tis_keys = jnp.concatenate([tis_own_s[own_at(index)], tis_side_s[side_at(index)]], axis=0)
        bias_s[...] = jnp.maximum(tis_keys, self_ref[...]) + win_ref[kind]

    def score_stage(index, pair):
        k_at, v_at = pair_cols(pair)
        bias = bias_s[...]
        scores = lax.dot_general(
            key_rows(index, k_at), split(q_ref[q_at(index), k_at]), dims(1, 1),
            preferred_element_type=f32,
        ) + jnp.concatenate([bias, bias], axis=1)
        x_s[pair][...] = scores
        top_s[pair][...] = jnp.max(scores, axis=0, keepdims=True)
        dp_s[pair][...] = lax.dot_general(
            key_rows(index, v_at), split(g_ref[q_at(index), k_at]), dims(1, 1),
            preferred_element_type=f32,
        )

    def softmax_stage(index, pair):
        top = top_s[pair][...]
        total = jnp.zeros((8, 2 * tile), f32)
        inner = jnp.zeros((8, 2 * tile), f32)
        fold = lambda a: jnp.sum(a.reshape(CHUNK // 8, 8, 2 * tile), axis=0)
        for begin in range(0, keys_all, CHUNK):
            at = slice(begin, begin + CHUNK)
            terms = jnp.exp(x_s[pair][at] - top)
            x_s[pair][at] = terms
            total = total + fold(terms)
            inner = inner + fold(terms * dp_s[pair][at])
        inverse = 1.0 / jnp.sum(total, axis=0, keepdims=True)
        delta = jnp.sum(inner, axis=0, keepdims=True) * inverse
        gate = tissue_ref[index].astype(f32)
        weight = inverse * jnp.concatenate([gate, gate], axis=1)
        for begin in range(0, keys_all, CHUNK):
            at = slice(begin, begin + CHUNK)
            probs = x_s[pair][at] * weight
            pl_s[pair][at] = probs.astype(bf16)
            sg_s[pair][at] = (probs * (dp_s[pair][at] - delta)).astype(bf16)

    def product_stage(index, pair):
        k_at, v_at = pair_cols(pair)
        keys = key_rows(index, k_at)
        values = key_rows(index, v_at)
        probs_low = pl_s[pair][...]
        score_grad = sg_s[pair][...]
        mix = joined(
            lax.dot_general(values, probs_low, dims(0, 0), preferred_element_type=f32)
        )
        att_t_s[k_at, q_at(index)] = mix.astype(bf16)
        att_ref[q_at(index), k_at] = mix.T.astype(bf16)
        dq = joined(lax.dot_general(keys, score_grad, dims(0, 0), preferred_element_type=f32))
        dq_ref[q_at(index), k_at] = (dq.T * FACTOR).astype(bf16)
        dk = jnp.dot(score_grad, split(q_ref[q_at(index), k_at]), preferred_element_type=f32)
        dv = jnp.dot(probs_low, split(g_ref[q_at(index), k_at]), preferred_element_type=f32)
        for grad, at in ((dk, k_at), (dv, v_at)):
            acc_own[own_at(index, 0, seen_own), at] += grad[:seen_own]
            acc_own[own_at(index, seen_own, tile), at] = grad[seen_own:own_keys]
            acc_side[side_at(index, 0, seen_side), at] += grad[own_keys : own_keys + seen_side]
            acc_side[side_at(index, seen_side, TILE_ROWS * SIDE), at] = grad[own_keys + seen_side :]

    make_bias(0)
    score_stage(0, 0)

    def step(index, carry):
        for pair in range(PAIRS):
            if pair + 1 < PAIRS:
                score_stage(index, pair + 1)
            else:
                later = jnp.minimum(index + 1, tiles - 1)
                make_bias(later)
                score_stage(later, 0)
            softmax_stage(index, pair)
            if pair > 0:
                product_stage(index, pair - 1)
            else:
                product_stage(jnp.maximum(index - 1, 0), PAIRS - 1)
        return carry

    lax.fori_loop(0, tiles, step, 0)
    product_stage(tiles - 1, PAIRS - 1)

    dkv_own_ref[...] = acc_own[...].astype(bf16)
    dkv_side_ref[...] = acc_side[...].astype(bf16)
    results = [
        pltpu.make_async_copy(source, target, sems.at[2 + i])
        for i, (source, target) in enumerate(
            [
                (dkv_own_ref, dkv_own_hbm),
                (att_ref, att_hbm),
                (dq_ref, dq_hbm),
            ]
        )
    ]
    for copy in results:
        copy.start()
    send_row = lax.broadcasted_iota(jnp.int32, (to_left_ref.shape[0], dkv_side_ref.shape[0]), 0)
    side_row = lax.broadcasted_iota(jnp.int32, send_row.shape, 1)
    for begin, send_ref in ((0, to_left_ref), (RADIUS, to_right_ref)):
        place = (send_row // (SIDE // 2)) * SIDE + send_row % (SIDE // 2) + begin
        pick = jnp.where(side_row == place, 1.0, 0.0).astype(bf16)
        send_ref[...] = jnp.dot(pick, dkv_side_ref[...], preferred_element_type=f32).astype(bf16)
    outside = jnp.concatenate(
        [above_ref[:, :width], below_ref[:, :width], side_ref[:, :width]], axis=0
    )

    def put(block, value):
        value = value.astype(bf16)
        for i in range(value.shape[1] // 128):
            part_ref[(block + i) * width : (block + i + 1) * width] = value[
                :, i * 128 : (i + 1) * 128
            ]

    columns = width // 128
    put(0, jnp.dot(tok_t_ref[...], dq_ref[...], preferred_element_type=f32))
    for begin in range(0, 2 * width, 256):
        at = slice(begin, begin + 256)
        grad_outside = jnp.concatenate(
            [dkv_own_ref[:halo, at], dkv_own_ref[halo + tokens_dev :, at], dkv_side_ref[:, at]],
            axis=0,
        )
        put(
            columns + begin // 128,
            jnp.dot(
                tok_t_ref[...],
                dkv_own_ref[halo : halo + tokens_dev, at],
                preferred_element_type=f32,
            )
            + lax.dot_general(outside, grad_outside, dims(0, 0), preferred_element_type=f32),
        )
    put(3 * columns, jnp.dot(att_t_s[...], cot_ref[...], preferred_element_type=f32))
    used = 4 * width * columns
    if used < part_ref.shape[0]:
        part_ref[used:] = jnp.zeros((part_ref.shape[0] - used, 128), bf16)
    for copy in results:
        copy.wait()


def attention(above, below, side, tok, cot, wp, wo, base, tissue, extents, rows_part):
    tokens_dev, width = cot.shape
    rows_own = tokens_dev + 2 * above.shape[0]
    rows_side = side.shape[0]
    tile = tissue.shape[2]
    keys_all = rows_own - tokens_dev + tile + KEY_ROWS * SIDE
    rows_send = -(-rows_side // 32) * 16
    vmem = pl.BlockSpec(memory_space=pltpu.VMEM)
    hbm = pl.BlockSpec(memory_space=pl.ANY)
    smem = pl.BlockSpec(memory_space=pltpu.SMEM)
    stage = []
    for shape, kind in (
        ((keys_all, 2 * tile), f32),
        ((keys_all, 2 * tile), f32),
        ((1, 2 * tile), f32),
        ((keys_all, 2 * tile), bf16),
        ((keys_all, 2 * tile), bf16),
    ):
        stage += [pltpu.VMEM(shape, kind)] * PAIRS
    return pl.pallas_call(
        functools.partial(attention_kernel, extents),
        out_shape=[
            jax.ShapeDtypeStruct((tokens_dev, width), bf16),
            jax.ShapeDtypeStruct((tokens_dev, width), bf16),
            jax.ShapeDtypeStruct((rows_own, 2 * width), bf16),
            jax.ShapeDtypeStruct((rows_send, 2 * width), bf16),
            jax.ShapeDtypeStruct((rows_send, 2 * width), bf16),
            jax.ShapeDtypeStruct((rows_part, 128), bf16),
        ],
        in_specs=[vmem] * 3 + [hbm] * 2 + [vmem] * 2 + [smem, vmem],
        out_specs=[hbm] * 3 + [vmem] * 3,
        scratch_shapes=[
            pltpu.VMEM((tokens_dev, width), bf16),
            pltpu.VMEM((tokens_dev, width), bf16),
            pltpu.VMEM((tokens_dev, width), bf16),
            pltpu.VMEM((tokens_dev, width), bf16),
            pltpu.VMEM((width, tokens_dev), bf16),
            pltpu.VMEM((tokens_dev, width), bf16),
            pltpu.VMEM((tokens_dev, width), bf16),
            pltpu.VMEM((rows_own, 2 * width), bf16),
            pltpu.VMEM((rows_side, 2 * width), bf16),
            pltpu.VMEM((rows_own, 2 * width), bf16),
            pltpu.VMEM((rows_side, 2 * width), bf16),
            pltpu.VMEM((rows_own, tile), f32),
            pltpu.VMEM((rows_side, tile), f32),
            pltpu.VMEM((keys_all, tile), f32),
            pltpu.VMEM((3, keys_all, tile), f32),
            pltpu.VMEM((keys_all, tile), f32),
            pltpu.VMEM((width, tokens_dev), bf16),
            pltpu.VMEM((rows_own, 2 * width), f32),
            pltpu.VMEM((rows_side, 2 * width), f32),
            pltpu.SemaphoreType.DMA((5,)),
        ]
        + stage,
        compiler_params=pltpu.CompilerParams(vmem_limit_bytes=56 * MIB),
        name="attention",
    )(above, below, side, tok, cot, wp, wo, base, tissue)


def to_next(array, axis):
    count = lax.axis_size(axis)
    return lax.ppermute(array, axis, [(i, (i + 1) % count) for i in range(count)])


def to_last(array, axis):
    count = lax.axis_size(axis)
    return lax.ppermute(array, axis, [((i + 1) % count, i) for i in range(count)])


def sum_kernel(pieces, pieces_ref, copies_ref):
    rows = pieces_ref.shape[0] // pieces
    pair = 2 * rows
    total = jnp.zeros((pair, 128), f32)
    for i in range(pieces // 2):
        total = total + pieces_ref[i * pair : (i + 1) * pair].astype(f32)
    total = total[:rows] + total[rows:]
    total = jnp.concatenate([total, total], axis=0).astype(bf16)
    for i in range(pieces // 2):
        copies_ref[i * pair : (i + 1) * pair] = total


def summed_copies(pieces, count):
    return pl.pallas_call(
        functools.partial(sum_kernel, count),
        out_shape=jax.ShapeDtypeStruct(pieces.shape, bf16),
        compiler_params=pltpu.CompilerParams(vmem_limit_bytes=16 * MIB),
        name="summed_copies",
    )(pieces)


def total_over_devices(partial):
    axes = ("row", "col")
    count = lax.axis_size("row") * lax.axis_size("col")
    pieces = lax.all_to_all(partial.reshape(count, -1, 128), axes, 0, 0, tiled=True)
    copies = summed_copies(pieces.reshape(partial.shape), count).reshape(pieces.shape)
    return lax.all_to_all(copies, axes, 0, 0, tiled=True).reshape(partial.shape)


def unpack_kernel(scale, whole_ref, packed_ref, output_ref):
    width = output_ref.shape[0]
    for block in range((packed_ref.shape[1] + output_ref.shape[1]) // 128):
        value = whole_ref[block * width : (block + 1) * width].astype(f32) * scale
        column = block * 128
        if column < packed_ref.shape[1]:
            packed_ref[:, column : column + 128] = value
        else:
            column -= packed_ref.shape[1]
            output_ref[:, column : column + 128] = value


def unpack(whole, width, scale):
    return pl.pallas_call(
        functools.partial(unpack_kernel, scale),
        out_shape=[
            jax.ShapeDtypeStruct((width, 3 * width), f32),
            jax.ShapeDtypeStruct((width, width), f32),
        ],
        compiler_params=pltpu.CompilerParams(vmem_limit_bytes=24 * MIB),
        name="unpack",
    )(whole)


def per_device(tokens, tissue, cotangent, packed_weight, output_weight):
    rows_dev, cols_dev, width = tokens.shape
    ext_rows = rows_dev + 2 * RADIUS
    devices = lax.axis_size("row") * lax.axis_size("col")
    rows_part = -(-4 * width * (width // 128) // (8 * devices)) * 8 * devices
    tile = TILE_ROWS * cols_dev
    total_scale = float(rows_dev * lax.axis_size("row") * cols_dev * lax.axis_size("col")) ** (-0.5)
    token_rows = tokens.reshape(-1, width)
    cotangent_rows = cotangent.reshape(-1, width)

    with_tissue = lambda a, b: jnp.concatenate([a, b.astype(bf16)[..., None]], axis=-1)
    above = to_next(with_tissue(tokens[-RADIUS:], tissue[-RADIUS:]), "row")
    below = to_last(with_tissue(tokens[:RADIUS], tissue[:RADIUS]), "row")
    left_cols = with_tissue(tokens[:, :RADIUS], tissue[:, :RADIUS])
    right_cols = with_tissue(tokens[:, -RADIUS:], tissue[:, -RADIUS:])
    left_cols = jnp.concatenate([above[:, :RADIUS], left_cols, below[:, :RADIUS]], axis=0)
    right_cols = jnp.concatenate([above[:, -RADIUS:], right_cols, below[:, -RADIUS:]], axis=0)
    from_left = to_next(right_cols, "col")
    from_right = to_last(left_cols, "col")
    pad = jnp.zeros((ext_rows, SIDE - 2 * RADIUS, width + 1), bf16)
    side = jnp.concatenate([from_left, from_right, pad], axis=1).reshape(-1, width + 1)

    base = jnp.stack([lax.axis_index("row") * rows_dev, lax.axis_index("col") * cols_dev])
    attended, dq, dkv_own, to_left, to_right, partial = attention(
        above.reshape(-1, width + 1), below.reshape(-1, width + 1), side,
        token_rows, cotangent_rows, packed_weight, output_weight,
        base.astype(jnp.int32), tissue.reshape(-1, 1, tile),
        (rows_dev * lax.axis_size("row"), cols_dev * lax.axis_size("col")), rows_part,
    )

    half = SIDE // 2

    def columns(sent):
        return sent[: ext_rows * half].reshape(ext_rows, half, 2 * width)[:, :RADIUS]

    from_right = columns(to_last(to_left, "col"))
    from_left = columns(to_next(to_right, "col"))
    dkv_own = dkv_own.reshape(ext_rows, cols_dev, 2 * width)
    first, last, inner = slice(None, RADIUS), slice(-RADIUS, None), slice(RADIUS, -RADIUS)

    def with_columns(rows):
        between = jnp.zeros((dkv_own[rows].shape[0], cols_dev - 2 * RADIUS, 2 * width), bf16)
        beside = jnp.concatenate([from_left[rows], between, from_right[rows]], axis=1)
        return dkv_own[rows].astype(f32) + beside.astype(f32)

    from_below = to_last(with_columns(first).astype(bf16), "row")
    from_above = to_next(with_columns(last).astype(bf16), "row")
    between = jnp.zeros((rows_dev - 2 * RADIUS, cols_dev, 2 * width), bf16)
    beside = jnp.concatenate([from_above, between, from_below], axis=0)
    dkv = with_columns(inner) + beside.astype(f32)
    dkv = dkv.astype(bf16).reshape(-1, 2 * width)

    contract = functools.partial(lax.dot_general, preferred_element_type=f32)
    layer_out = (
        token_rows.astype(f32) + jnp.dot(attended, output_weight, preferred_element_type=f32)
    ).astype(bf16)
    grad_tokens = (
        cotangent_rows.astype(f32)
        + contract(dq, packed_weight[:, :width], dims(1, 1))
        + contract(dkv, packed_weight[:, width:], dims(1, 1))
    ).astype(bf16)
    grad_packed, grad_output = unpack(total_over_devices(partial), width, total_scale)
    return (
        layer_out.reshape(rows_dev, cols_dev, width),
        grad_tokens.reshape(rows_dev, cols_dev, width),
        grad_packed,
        grad_output,
    )


def solution(mesh):
    in_specs = (P("row", "col", None), P("row", "col"), P("row", "col", None), P(), P())
    out_specs = (P("row", "col", None), P("row", "col", None), P(), P())
    return jax.shard_map(
        per_device, mesh=mesh, in_specs=in_specs, out_specs=out_specs, check_vma=False
    )
```

```python
import functools

import jax
import jax.numpy as jnp
from jax import lax
from jax.experimental import pallas as pl
from jax.experimental.pallas import tpu as pltpu
from jax.sharding import PartitionSpec as P

HEADS = 6
HEAD = 64
KERNEL = 7
RADIUS = 3
PAIR = 2 * HEAD
PAIRS = HEADS // 2
SIDE = 8
TILE_ROWS = 4
KEY_ROWS = TILE_ROWS + 2 * RADIUS
CHUNK = 48
SPAN = 2
PROJECT_TILES = 4
FACTOR = HEAD ** (-0.5)
NEG = float("-inf")
MIB = 1024 * 1024
f32 = jnp.float32
bf16 = jnp.bfloat16


def dims(lhs, rhs):
    return (((lhs,), (rhs,)), ((), ()))


def project_kernel(
    tok_ref, cot_ref, wp_ref, wo_ref, tissue_ref, q_ref, kv_ref, g_ref, tok_t_ref, tis_ref
):
    width = tok_ref.shape[1]
    tile = tis_ref.shape[1]
    tok = tok_ref[...]
    q = jnp.dot(tok, wp_ref[:, :width], preferred_element_type=f32).astype(bf16)
    q_ref[...] = (q * FACTOR).astype(bf16)
    kv_ref[...] = jnp.dot(tok, wp_ref[:, width:], preferred_element_type=f32).astype(bf16)
    g_ref[...] = lax.dot_general(
        cot_ref[...], wo_ref[...], dims(1, 1), preferred_element_type=f32
    ).astype(bf16)
    tok_t_ref[...] = tok.T
    for i in range(tissue_ref.shape[0]):
        across = jnp.broadcast_to(tissue_ref[i].astype(f32), (tile, tile)).T
        tis_ref[i * tile : (i + 1) * tile] = jnp.where(across > 0.5, 0.0, NEG)


def project(tok, cot, wp, wo, tissue):
    count, width = tok.shape
    tile = tissue.shape[2]
    rows = PROJECT_TILES * tile
    block = lambda cols: pl.BlockSpec((rows, cols), lambda i: (i, 0))
    whole = lambda a: pl.BlockSpec(a.shape, lambda i: (0, 0))
    return pl.pallas_call(
        project_kernel,
        grid=(count // rows,),
        out_shape=[
            jax.ShapeDtypeStruct((count, width), bf16),
            jax.ShapeDtypeStruct((count, 2 * width), bf16),
            jax.ShapeDtypeStruct((count, width), bf16),
            jax.ShapeDtypeStruct((width, count), bf16),
            jax.ShapeDtypeStruct((count, tile), f32),
        ],
        in_specs=[
            block(width),
            block(width),
            whole(wp),
            whole(wo),
            pl.BlockSpec((PROJECT_TILES, 1, tile), lambda i: (i, 0, 0)),
        ],
        out_specs=[
            block(width),
            block(2 * width),
            block(width),
            pl.BlockSpec((width, rows), lambda i: (0, i)),
            block(tile),
        ],
        compiler_params=pltpu.CompilerParams(vmem_limit_bytes=56 * MIB),
        cost_estimate=pl.CostEstimate(
            flops=2 * count * width * 4 * width, bytes_accessed=14 * count * width, transcendentals=0
        ),
        name="project",
    )(tok, cot, wp, wo, tissue)


def attention_kernel(
    extents,
    above_ref, below_ref, side_ref, q_hbm, kv_hbm, g_hbm, tis_hbm, tok_t_hbm, cot_hbm, wp_ref, base_ref,
    tissue_ref,
    att_hbm, dq_hbm, dkv_own_hbm, to_left_ref, to_right_ref, part_ref,
    cot_ref, q_ref, g_ref, tok_t_ref, att_ref, dq_ref, dkv_own_ref, dkv_side_ref,
    kv_own_s, kv_aux_s, tis_own_s, tis_aux_s, win_s, self_s, gate_s, acc_own, acc_aux, sems, *stage,
):
    tokens_dev, width = q_ref.shape
    halo = above_ref.shape[0]
    rows_own = tokens_dev + 2 * halo
    rows_aux = side_ref.shape[0]
    cols = halo // RADIUS
    wide = cols // 2
    tile = TILE_ROWS * wide
    band = TILE_ROWS * cols
    bands = tokens_dev // band
    own_keys = KEY_ROWS * wide
    aux_keys = KEY_ROWS * SIDE
    keys_all = own_keys + aux_keys
    most = 4 * HEAD
    x_s, dp_s, top_s, pl_s, sg_s = (stage[2 * i : 2 * i + 2] for i in range(5))

    middle = pl.ds(halo, tokens_dev)
    copies = [
        pltpu.make_async_copy(source, target, sems.at[i])
        for i, (source, target) in enumerate(
            [
                (kv_hbm, kv_own_s.at[middle]),
                (tis_hbm, tis_own_s.at[middle]),
                (q_hbm, q_ref),
                (g_hbm, g_ref),
                (tok_t_hbm, tok_t_ref),
                (cot_hbm, cot_ref),
            ]
        )
    ]
    for copy in copies:
        copy.start()

    def lanes(column):
        bias = jnp.where(column.astype(f32) > 0.5, 0.0, NEG)
        return jnp.broadcast_to(bias, (bias.shape[0], 2 * tile))

    def outer(rows_ref):
        return jnp.dot(
            rows_ref[:, :width], wp_ref[:, width:], preferred_element_type=f32
        ).astype(bf16)

    kv_own_s[:halo] = outer(above_ref)
    kv_own_s[halo + tokens_dev :] = outer(below_ref)
    kv_side = outer(side_ref)
    tis_own_s[:halo] = lanes(above_ref[:, width : width + 1])
    tis_own_s[halo + tokens_dev :] = lanes(below_ref[:, width : width + 1])
    tis_side = lanes(side_ref[:, width : width + 1])

    lane = lax.broadcasted_iota(jnp.int32, (1, 2 * tile), 1) % tile
    query_row = lane // wide
    query_col = lane % wide

    def window(key, query, base, extent):
        start = jnp.clip(base + query - RADIUS, 0, extent - KERNEL) - base
        return jnp.where((key >= start) & (key < start + KERNEL), 0.0, NEG)

    own_col = lax.broadcasted_iota(jnp.int32, (wide, 2 * tile), 0)
    aux_place = lax.broadcasted_iota(jnp.int32, (SIDE, 2 * tile), 0)
    far = -(2**20)
    first_in = jnp.where(aux_place < RADIUS, aux_place - RADIUS, aux_place - RADIUS + wide)
    second_in = jnp.where(
        aux_place < RADIUS, aux_place - RADIUS + wide, aux_place - RADIUS + cols
    )
    for half, aux_col in enumerate((first_in, second_in)):
        aux_col = jnp.where(aux_place < 2 * RADIUS, aux_col, far)
        shift = half * wide
        own_in = window(own_col + shift, query_col + shift, base_ref[1], extents[1])
        aux_in = window(aux_col, query_col + shift, base_ref[1], extents[1])
        own_same = jnp.where(own_col == query_col, 0.0, NEG)
        for key_row in range(KEY_ROWS):
            own_rows = slice(key_row * wide, (key_row + 1) * wide)
            aux_rows = slice(own_keys + key_row * SIDE, own_keys + (key_row + 1) * SIDE)
            for kind, first in enumerate((0, 2 * TILE_ROWS, (bands - 1) * TILE_ROWS)):
                row_in = window(key_row - RADIUS, query_row, base_ref[0] + first, extents[0])
                win_s[half, kind, own_rows] = own_in + row_in
                win_s[half, kind, aux_rows] = aux_in + row_in
            if half == 0:
                row_same = jnp.where(query_row == key_row - RADIUS, 0.0, NEG)
                self_s[own_rows] = own_same + row_same
                self_s[aux_rows] = jnp.full((SIDE, 2 * tile), NEG, f32)
    tissue = tissue_ref[...].astype(f32)
    for index in range(bands):
        for half in range(2):
            pieces = [
                tissue[
                    index * TILE_ROWS + row : index * TILE_ROWS + row + 1,
                    half * wide : (half + 1) * wide,
                ]
                for row in range(TILE_ROWS)
            ]
            gate_s[2 * index + half] = jnp.concatenate(pieces * 2, axis=1)

    place = lax.broadcasted_iota(jnp.int32, (rows_aux, 1), 0) % SIDE
    outer_left, outer_right = place < RADIUS, (place >= RADIUS) & (place < 2 * RADIUS)

    def parts(array, begin, count):
        across = array.shape[1]
        return array.reshape(rows_own // cols, cols, across)[:, begin : begin + count].reshape(
            -1, across
        )

    def with_inner(own, side):
        first = parts(own, wide, SIDE)
        second = parts(own, wide - SIDE, SIDE)
        return (
            jnp.where(outer_left, side, pltpu.roll(first, RADIUS, 0)),
            jnp.where(outer_right, side, pltpu.roll(second, rows_aux - SIDE + RADIUS, 0)),
        )

    for copy in copies[:2]:
        copy.wait()
    tis_aux_s[0], tis_aux_s[1] = with_inner(tis_own_s[...], tis_side)
    for begin in range(0, 2 * width, 256):
        at = slice(begin, begin + 256)
        one, two = with_inner(kv_own_s[:, at].astype(f32), kv_side[:, at].astype(f32))
        kv_aux_s[0, :, at] = one.astype(bf16)
        kv_aux_s[1, :, at] = two.astype(bf16)
    seen_rows = KEY_ROWS - TILE_ROWS
    acc_own[: seen_rows * cols] = jnp.zeros((seen_rows * cols, 2 * width), f32)
    acc_aux[:, : seen_rows * SIDE] = jnp.zeros((2, seen_rows * SIDE, 2 * width), f32)
    pl_s[1][...] = jnp.zeros((keys_all, HEADS * tile), bf16)
    sg_s[1][...] = jnp.zeros((keys_all, HEADS * tile), bf16)
    for copy in copies[2:4]:
        copy.wait()

    def split(block):
        head = lax.broadcasted_iota(jnp.int32, block.shape, 1) // HEAD
        zero = jnp.zeros_like(block)
        return jnp.concatenate(
            [jnp.where(head == i, block, zero) for i in range(block.shape[1] // HEAD)], axis=0
        )

    def corner(one, two):
        zero = jnp.zeros_like(one)
        return jnp.concatenate(
            [jnp.concatenate([one, zero], axis=1), jnp.concatenate([zero, two], axis=1)], axis=0
        )

    def own_at(index, half, row):
        return pl.ds(pl.multiple_of(index * band, band) + row * cols + half * wide, wide)

    def aux_at(index, begin, count):
        step = TILE_ROWS * SIDE
        return pl.ds(pl.multiple_of(index * step, step) + begin * SIDE, count * SIDE)

    def queries(ref, index, half):
        return jnp.concatenate([ref[own_at(index, half, row), :] for row in range(TILE_ROWS)], axis=0)

    def key_rows(index, half, at):
        rows = [kv_own_s[own_at(index, half, row), at] for row in range(KEY_ROWS)]
        return jnp.concatenate(rows + [kv_aux_s[half, aux_at(index, 0, KEY_ROWS), at]], axis=0)

    def score_stage(index, half):
        kind = jnp.where(index == 0, 0, jnp.where(index == bands - 1, 2, 1))
        tis_keys = jnp.concatenate(
            [tis_own_s[own_at(index, half, row)] for row in range(KEY_ROWS)]
            + [tis_aux_s[half, aux_at(index, 0, KEY_ROWS)]],
            axis=0,
        )
        bias = jnp.maximum(tis_keys, self_s[...]) + win_s[half, kind]
        q, g = queries(q_ref, index, half), queries(g_ref, index, half)
        keys = key_rows(index, half, slice(0, width))
        values = key_rows(index, half, slice(width, 2 * width))
        product = functools.partial(
            lax.dot_general, dimension_numbers=dims(1, 1), preferred_element_type=f32
        )
        rest = product(
            jnp.concatenate([keys[:, most:], values[:, most:]], axis=1),
            corner(split(q[:, most:]), split(g[:, most:])),
        )
        cut = HEADS * tile - 4 * tile
        scores = jnp.concatenate(
            [product(keys[:, :most], split(q[:, :most])), rest[:, :cut]], axis=1
        )
        scores = scores + jnp.concatenate([bias] * PAIRS, axis=1)
        x_s[half][...] = scores
        top_s[half][...] = jnp.max(scores, axis=0, keepdims=True)
        dp_s[half][:, : 4 * tile] = product(values[:, :most], split(g[:, :most]))
        dp_s[half][:, 4 * tile :] = rest[:, cut:]

    def softmax_stage(index, half):
        top = top_s[half][...]
        total = jnp.zeros((8, HEADS * tile), f32)
        inner = jnp.zeros((8, HEADS * tile), f32)
        fold = lambda a: jnp.sum(a.reshape(CHUNK // 8, 8, HEADS * tile), axis=0)
        for begin in range(0, keys_all, CHUNK):
            at = slice(begin, begin + CHUNK)
            terms = jnp.exp(x_s[half][at] - top)
            x_s[half][at] = terms
            total = total + fold(terms)
            inner = inner + fold(terms * dp_s[half][at])
        inverse = 1.0 / jnp.sum(total, axis=0, keepdims=True)
        delta = jnp.sum(inner, axis=0, keepdims=True) * inverse
        weight = inverse * jnp.concatenate([gate_s[2 * index + half]] * PAIRS, axis=1)
        for begin in range(0, keys_all, CHUNK):
            at = slice(begin, begin + CHUNK)
            probs = x_s[half][at] * weight
            pl_s[half][at] = probs.astype(bf16)
            sg_s[half][at] = (probs * (dp_s[half][at] - delta)).astype(bf16)

    def product_stage(index, half):
        keys = key_rows(index, half, slice(0, width))
        values = key_rows(index, half, slice(width, 2 * width))
        probs_low = pl_s[half][...]
        score_grad = sg_s[half][...]
        first_head = lax.broadcasted_iota(jnp.int32, (tile, PAIR), 1) < HEAD
        for pair in range(PAIRS):
            at = slice(pair * PAIR, (pair + 1) * PAIR)
            for rows, weight, scale, out_ref in (
                (values, probs_low, 1.0, att_ref),
                (keys, score_grad, FACTOR, dq_ref),
            ):
                both = lax.dot_general(
                    rows[:, at], weight[:, at], dims(0, 0), preferred_element_type=f32
                ).T
                mixed = (jnp.where(first_head, both[:tile], both[tile:]) * scale).astype(bf16)
                for row in range(TILE_ROWS):
                    out_ref[own_at(index, half, row), at] = mixed[row * wide : (row + 1) * wide]
        q, g = queries(q_ref, index, half), queries(g_ref, index, half)
        rest = jnp.dot(
            jnp.concatenate([probs_low[:, 4 * tile :], score_grad[:, 4 * tile :]], axis=1),
            corner(split(g[:, most:]), split(q[:, most:])),
            preferred_element_type=f32,
        )
        cut = width - most
        dk = jnp.dot(score_grad[:, : 4 * tile], split(q[:, :most]), preferred_element_type=f32)
        dv = jnp.dot(probs_low[:, : 4 * tile], split(g[:, :most]), preferred_element_type=f32)
        for grad, at in (
            (dk, slice(0, most)),
            (rest[:, cut:], slice(most, width)),
            (dv, slice(width, width + most)),
            (rest[:, :cut], slice(width + most, 2 * width)),
        ):
            for row in range(KEY_ROWS):
                piece = grad[row * wide : (row + 1) * wide]
                if row < seen_rows:
                    acc_own[own_at(index, half, row), at] += piece
                else:
                    acc_own[own_at(index, half, row), at] = piece
            seen = own_keys + seen_rows * SIDE
            acc_aux[half, aux_at(index, 0, seen_rows), at] += grad[own_keys:seen]
            acc_aux[half, aux_at(index, seen_rows, TILE_ROWS), at] = grad[seen:]

    score_stage(0, 0)

    def step(group, carry):
        for slot in range(2 * SPAN):
            index = group * SPAN + slot // 2
            half = slot % 2
            if half == 0:
                product_stage(jnp.maximum(index - 1, 0), 1)
            else:
                product_stage(index, 0)
            softmax_stage(index, half)
            if half == 0:
                score_stage(index, 1)
            else:
                score_stage(jnp.minimum(index + 1, bands - 1), 0)
        return carry

    lax.fori_loop(0, bands // SPAN, step, 0)
    product_stage(bands - 1, 1)

    for begin in range(0, 2 * width, 128):
        at = slice(begin, begin + 128)
        one, two = acc_aux[0, :, at], acc_aux[1, :, at]
        dkv_side_ref[:, at] = jnp.where(
            outer_left, one, jnp.where(outer_right, two, 0.0)
        ).astype(bf16)
        first = jnp.where(place < RADIUS, pltpu.roll(one, rows_aux - RADIUS, 0), 0.0)
        second = jnp.where(
            place >= SIDE - RADIUS, pltpu.roll(two, SIDE - RADIUS, 0), 0.0
        )
        shape = (rows_aux // SIDE, SIDE, 128)
        blank = lambda count: jnp.zeros((shape[0], count, 128), f32)
        inner = jnp.concatenate(
            [
                blank(wide - SIDE),
                second.reshape(shape),
                first.reshape(shape),
                blank(cols - wide - SIDE),
            ],
            axis=1,
        ).reshape(rows_own, 128)
        dkv_own_ref[:, at] = (acc_own[:, at] + inner).astype(bf16)
    results = [
        pltpu.make_async_copy(source, target, sems.at[6 + i])
        for i, (source, target) in enumerate(
            [(dkv_own_ref, dkv_own_hbm), (att_ref, att_hbm), (dq_ref, dq_hbm)]
        )
    ]
    for copy in results:
        copy.start()
    for copy in copies[4:]:
        copy.wait()
    send_row = lax.broadcasted_iota(jnp.int32, (128, 256), 0)
    side_row = lax.broadcasted_iota(jnp.int32, (128, 256), 1)
    place = (send_row // (SIDE // 2)) * SIDE + send_row % (SIDE // 2)
    for begin, send_ref in ((0, to_left_ref), (RADIUS, to_right_ref)):
        pick = jnp.where(side_row == place + begin, 1.0, 0.0).astype(bf16)
        for first in range(0, send_ref.shape[0], 128):
            count = min(128, send_ref.shape[0] - first)
            source = dkv_side_ref[2 * first : min(2 * (first + count), dkv_side_ref.shape[0])]
            send_ref[first : first + count] = jnp.dot(
                pick[:count, : source.shape[0]], source, preferred_element_type=f32
            ).astype(bf16)
    outside = jnp.concatenate(
        [above_ref[:, :width], below_ref[:, :width], side_ref[:, :width]], axis=0
    )

    def put(block, value):
        value = value.astype(bf16)
        for i in range(value.shape[1] // 128):
            part_ref[(block + i) * width : (block + i + 1) * width] = value[
                :, i * 128 : (i + 1) * 128
            ]

    columns = width // 128
    put(0, jnp.dot(tok_t_ref[...], dq_ref[...], preferred_element_type=f32))
    for begin in range(0, 2 * width, 256):
        at = slice(begin, begin + 256)
        grad_outside = jnp.concatenate(
            [dkv_own_ref[:halo, at], dkv_own_ref[halo + tokens_dev :, at], dkv_side_ref[:, at]],
            axis=0,
        )
        put(
            columns + begin // 128,
            jnp.dot(
                tok_t_ref[...],
                dkv_own_ref[halo : halo + tokens_dev, at],
                preferred_element_type=f32,
            )
            + lax.dot_general(outside, grad_outside, dims(0, 0), preferred_element_type=f32),
        )
    put(3 * columns, lax.dot_general(
            att_ref[...], cot_ref[...], dims(0, 0), preferred_element_type=f32
        ))
    used = 4 * width * columns
    if used < part_ref.shape[0]:
        part_ref[used:] = jnp.zeros((part_ref.shape[0] - used, 128), bf16)
    for copy in results:
        copy.wait()


def attention(
    above, below, side, q, kv, g, tis, tok_t, cot, wp, base, tissue, extents, rows_part
):
    tokens_dev, width = cot.shape
    rows_own = tokens_dev + 2 * above.shape[0]
    rows_side = side.shape[0]
    cols = tissue.shape[1]
    tile = TILE_ROWS * cols // 2
    keys_all = KEY_ROWS * (cols // 2 + SIDE)
    rows_send = -(-rows_side // 32) * 16
    vmem = pl.BlockSpec(memory_space=pltpu.VMEM)
    hbm = pl.BlockSpec(memory_space=pl.ANY)
    smem = pl.BlockSpec(memory_space=pltpu.SMEM)
    stage = []
    for shape, kind in (
        ((keys_all, HEADS * tile), f32),
        ((keys_all, HEADS * tile), f32),
        ((1, HEADS * tile), f32),
        ((keys_all, HEADS * tile), bf16),
        ((keys_all, HEADS * tile), bf16),
    ):
        stage += [pltpu.VMEM(shape, kind)] * 2
    return pl.pallas_call(
        functools.partial(attention_kernel, extents),
        out_shape=[
            jax.ShapeDtypeStruct((tokens_dev, width), bf16),
            jax.ShapeDtypeStruct((tokens_dev, width), bf16),
            jax.ShapeDtypeStruct((rows_own, 2 * width), bf16),
            jax.ShapeDtypeStruct((rows_send, 2 * width), bf16),
            jax.ShapeDtypeStruct((rows_send, 2 * width), bf16),
            jax.ShapeDtypeStruct((rows_part, 128), bf16),
        ],
        in_specs=[vmem] * 3 + [hbm] * 6 + [vmem, smem, vmem],
        out_specs=[hbm] * 3 + [vmem] * 3,
        scratch_shapes=[
            pltpu.VMEM((tokens_dev, width), bf16),
            pltpu.VMEM((tokens_dev, width), bf16),
            pltpu.VMEM((tokens_dev, width), bf16),
            pltpu.VMEM((width, tokens_dev), bf16),
            pltpu.VMEM((tokens_dev, width), bf16),
            pltpu.VMEM((tokens_dev, width), bf16),
            pltpu.VMEM((rows_own, 2 * width), bf16),
            pltpu.VMEM((rows_side, 2 * width), bf16),
            pltpu.VMEM((rows_own, 2 * width), bf16),
            pltpu.VMEM((2, rows_side, 2 * width), bf16),
            pltpu.VMEM((rows_own, 2 * tile), f32),
            pltpu.VMEM((2, rows_side, 2 * tile), f32),
            pltpu.VMEM((2, 3, keys_all, 2 * tile), f32),
            pltpu.VMEM((keys_all, 2 * tile), f32),
            pltpu.VMEM((2 * tokens_dev // (2 * tile), 1, 2 * tile), f32),
            pltpu.VMEM((rows_own, 2 * width), f32),
            pltpu.VMEM((2, rows_side, 2 * width), f32),
            pltpu.SemaphoreType.DMA((9,)),
        ]
        + stage,
        compiler_params=pltpu.CompilerParams(vmem_limit_bytes=56 * MIB),
        name="attention",
    )(above, below, side, q, kv, g, tis, tok_t, cot, wp, base, tissue)


def to_next(array, axis):
    count = lax.axis_size(axis)
    return lax.ppermute(array, axis, [(i, (i + 1) % count) for i in range(count)])


def to_last(array, axis):
    count = lax.axis_size(axis)
    return lax.ppermute(array, axis, [((i + 1) % count, i) for i in range(count)])


def sum_kernel(pieces, pieces_ref, copies_ref):
    rows = pieces_ref.shape[0] // pieces
    pair = 2 * rows
    total = jnp.zeros((pair, 128), f32)
    for i in range(pieces // 2):
        total = total + pieces_ref[i * pair : (i + 1) * pair].astype(f32)
    total = total[:rows] + total[rows:]
    total = jnp.concatenate([total, total], axis=0).astype(bf16)
    for i in range(pieces // 2):
        copies_ref[i * pair : (i + 1) * pair] = total


def summed_copies(pieces, count):
    return pl.pallas_call(
        functools.partial(sum_kernel, count),
        out_shape=jax.ShapeDtypeStruct(pieces.shape, bf16),
        compiler_params=pltpu.CompilerParams(vmem_limit_bytes=16 * MIB),
        name="summed_copies",
    )(pieces)


def total_over_devices(partial):
    axes = ("row", "col")
    count = lax.axis_size("row") * lax.axis_size("col")
    pieces = lax.all_to_all(partial.reshape(count, -1, 128), axes, 0, 0, tiled=True)
    copies = summed_copies(pieces.reshape(partial.shape), count).reshape(pieces.shape)
    return lax.all_to_all(copies, axes, 0, 0, tiled=True).reshape(partial.shape)


def unpack_kernel(scale, whole_ref, packed_ref, output_ref):
    width = output_ref.shape[0]
    for block in range((packed_ref.shape[1] + output_ref.shape[1]) // 128):
        value = whole_ref[block * width : (block + 1) * width].astype(f32) * scale
        column = block * 128
        if column < packed_ref.shape[1]:
            packed_ref[:, column : column + 128] = value
        else:
            column -= packed_ref.shape[1]
            output_ref[:, column : column + 128] = value


def unpack(whole, width, scale):
    return pl.pallas_call(
        functools.partial(unpack_kernel, scale),
        out_shape=[
            jax.ShapeDtypeStruct((width, 3 * width), f32),
            jax.ShapeDtypeStruct((width, width), f32),
        ],
        compiler_params=pltpu.CompilerParams(vmem_limit_bytes=24 * MIB),
        name="unpack",
    )(whole)


def per_device(tokens, tissue, cotangent, packed_weight, output_weight):
    rows_dev, cols_dev, width = tokens.shape
    ext_rows = rows_dev + 2 * RADIUS
    devices = lax.axis_size("row") * lax.axis_size("col")
    rows_part = -(-4 * width * (width // 128) // (8 * devices)) * 8 * devices
    tile = TILE_ROWS * cols_dev
    total_scale = float(rows_dev * lax.axis_size("row") * cols_dev * lax.axis_size("col")) ** (-0.5)
    token_rows = tokens.reshape(-1, width)
    cotangent_rows = cotangent.reshape(-1, width)

    with_tissue = lambda a, b: jnp.concatenate([a, b.astype(bf16)[..., None]], axis=-1)
    above = to_next(with_tissue(tokens[-RADIUS:], tissue[-RADIUS:]), "row")
    below = to_last(with_tissue(tokens[:RADIUS], tissue[:RADIUS]), "row")
    left_cols = with_tissue(tokens[:, :RADIUS], tissue[:, :RADIUS])
    right_cols = with_tissue(tokens[:, -RADIUS:], tissue[:, -RADIUS:])
    left_cols = jnp.concatenate([above[:, :RADIUS], left_cols, below[:, :RADIUS]], axis=0)
    right_cols = jnp.concatenate([above[:, -RADIUS:], right_cols, below[:, -RADIUS:]], axis=0)
    tiles = tissue.reshape(-1, 1, tile)
    token_rows, left_cols, right_cols = lax.optimization_barrier(
        (token_rows, left_cols, right_cols)
    )
    from_left = to_next(right_cols, "col")
    from_right = to_last(left_cols, "col")
    pad = jnp.zeros((ext_rows, SIDE - 2 * RADIUS, width + 1), bf16)
    side = jnp.concatenate([from_left, from_right, pad], axis=1).reshape(-1, width + 1)

    q, kv, g, tok_t, tis = project(
        token_rows, cotangent_rows, packed_weight, output_weight, tiles
    )
    base = jnp.stack([lax.axis_index("row") * rows_dev, lax.axis_index("col") * cols_dev])
    attended, dq, dkv_own, to_left, to_right, partial = attention(
        above.reshape(-1, width + 1), below.reshape(-1, width + 1), side,
        q, kv, g, tis, tok_t, cotangent_rows, packed_weight, base.astype(jnp.int32), tissue,
        (rows_dev * lax.axis_size("row"), cols_dev * lax.axis_size("col")), rows_part,
    )

    half = SIDE // 2

    def columns(sent):
        return sent[: ext_rows * half].reshape(ext_rows, half, 2 * width)[:, :RADIUS]

    from_right = columns(to_last(to_left, "col"))
    from_left = columns(to_next(to_right, "col"))
    dkv_own = dkv_own.reshape(ext_rows, cols_dev, 2 * width)
    first, last, inner = slice(None, RADIUS), slice(-RADIUS, None), slice(RADIUS, -RADIUS)

    def with_columns(rows):
        between = jnp.zeros((dkv_own[rows].shape[0], cols_dev - 2 * RADIUS, 2 * width), bf16)
        beside = jnp.concatenate([from_left[rows], between, from_right[rows]], axis=1)
        return dkv_own[rows].astype(f32) + beside.astype(f32)

    from_below = to_last(with_columns(first).astype(bf16), "row")
    from_above = to_next(with_columns(last).astype(bf16), "row")
    between = jnp.zeros((rows_dev - 2 * RADIUS, cols_dev, 2 * width), bf16)
    beside = jnp.concatenate([from_above, between, from_below], axis=0)
    dkv = with_columns(inner) + beside.astype(f32)
    dkv = dkv.astype(bf16).reshape(-1, 2 * width)

    contract = functools.partial(lax.dot_general, preferred_element_type=f32)
    layer_out = (
        token_rows.astype(f32) + jnp.dot(attended, output_weight, preferred_element_type=f32)
    ).astype(bf16)
    grad_tokens = (
        cotangent_rows.astype(f32)
        + contract(dq, packed_weight[:, :width], dims(1, 1))
        + contract(dkv, packed_weight[:, width:], dims(1, 1))
    ).astype(bf16)
    grad_packed, grad_output = unpack(total_over_devices(partial), width, total_scale)
    return (
        layer_out.reshape(rows_dev, cols_dev, width),
        grad_tokens.reshape(rows_dev, cols_dev, width),
        grad_packed,
        grad_output,
    )


def solution(mesh):
    in_specs = (P("row", "col", None), P("row", "col"), P("row", "col", None), P(), P())
    out_specs = (P("row", "col", None), P("row", "col", None), P(), P())
    return jax.shard_map(
        per_device, mesh=mesh, in_specs=in_specs, out_specs=out_specs, check_vma=False
    )
```

```python
import functools

import jax
import jax.numpy as jnp
from jax import lax
from jax.experimental import pallas as pl
from jax.experimental.pallas import tpu as pltpu
from jax.sharding import PartitionSpec as P

HEADS = 6
HEAD = 64
KERNEL = 7
RADIUS = 3
PAIR = 2 * HEAD
PAIRS = HEADS // 2
SIDE = 8
TILE_ROWS = 4
KEY_ROWS = TILE_ROWS + 2 * RADIUS
CHUNK = 48
SPAN = 2
PROJECT_STEPS = 2
FACTOR = HEAD ** (-0.5)
NEG = float("-inf")
MIB = 1024 * 1024
f32 = jnp.float32
bf16 = jnp.bfloat16


def dims(lhs, rhs):
    return (((lhs,), (rhs,)), ((), ()))


def project_kernel(
    tok_ref, cot_ref, wp_ref, wo_ref, q_ref, kv_ref, g_ref, tok_t_ref
):
    width = tok_ref.shape[1]
    tok = tok_ref[...]
    q = jnp.dot(tok, wp_ref[:, :width], preferred_element_type=f32).astype(bf16)
    q_ref[...] = (q * FACTOR).astype(bf16)
    kv_ref[...] = jnp.dot(tok, wp_ref[:, width:], preferred_element_type=f32).astype(bf16)
    g_ref[...] = lax.dot_general(
        cot_ref[...], wo_ref[...], dims(1, 1), preferred_element_type=f32
    ).astype(bf16)
    tok_t_ref[...] = tok.T


def project(tok, cot, wp, wo):
    count, width = tok.shape
    rows = count // PROJECT_STEPS
    block = lambda cols: pl.BlockSpec((rows, cols), lambda i: (i, 0))
    whole = lambda a: pl.BlockSpec(a.shape, lambda i: (0, 0))
    return pl.pallas_call(
        project_kernel,
        grid=(count // rows,),
        out_shape=[
            jax.ShapeDtypeStruct((count, width), bf16),
            jax.ShapeDtypeStruct((count, 2 * width), bf16),
            jax.ShapeDtypeStruct((count, width), bf16),
            jax.ShapeDtypeStruct((width, count), bf16),
        ],
        in_specs=[block(width), block(width), whole(wp), whole(wo)],
        out_specs=[
            block(width),
            block(2 * width),
            block(width),
            pl.BlockSpec((width, rows), lambda i: (0, i)),
        ],
        compiler_params=pltpu.CompilerParams(vmem_limit_bytes=56 * MIB),
        cost_estimate=pl.CostEstimate(
            flops=2 * count * width * 4 * width, bytes_accessed=14 * count * width, transcendentals=0
        ),
        name="project",
    )(tok, cot, wp, wo)


def attention_kernel(
    extents,
    above_ref, below_ref, side_ref, q_hbm, kv_hbm, g_hbm, tok_t_hbm, cot_hbm, wp_ref, tissue_ref,
    att_hbm, dq_hbm, dkv_own_hbm, to_left_ref, to_right_ref, part_ref,
    cot_ref, q_ref, g_ref, tok_t_ref, att_ref, dq_ref, dkv_own_ref, dkv_side_ref,
    kv_own_s, kv_aux_s, tis_own_s, tis_aux_s, win_s, self_s, gate_s, acc_own, acc_aux, sems, *stage,
):
    tokens_dev, width = q_ref.shape
    halo = above_ref.shape[0]
    rows_own = tokens_dev + 2 * halo
    rows_aux = side_ref.shape[0]
    cols = halo // RADIUS
    wide = cols // 2
    tile = TILE_ROWS * wide
    band = TILE_ROWS * cols
    bands = tokens_dev // band
    own_keys = KEY_ROWS * wide
    aux_keys = KEY_ROWS * SIDE
    keys_all = own_keys + aux_keys
    most = 4 * HEAD
    x_s, dp_s, top_s, pl_s, sg_s = (stage[2 * i : 2 * i + 2] for i in range(5))

    part = tokens_dev // 2
    early = []
    for i in range(2):
        rows = pl.ds(i * part, part)
        targets = (kv_own_s.at[pl.ds(halo + i * part, part)], q_ref.at[rows], g_ref.at[rows])
        for k, (source, target) in enumerate(zip((kv_hbm, q_hbm, g_hbm), targets)):
            early.append(pltpu.make_async_copy(source.at[rows], target, sems.at[3 * i + k]))
    for copy in early:
        copy.start()
    late = [
        pltpu.make_async_copy(tok_t_hbm, tok_t_ref, sems.at[6]),
        pltpu.make_async_copy(cot_hbm, cot_ref, sems.at[7]),
    ]
    done = tokens_dev // 2
    results = []
    for i in range(2):
        rows = pl.ds(i * done, done)
        ext = rows if i == 0 else pl.ds(done, rows_own - done)
        for k, (source, target, at) in enumerate(
            [
                (att_ref, att_hbm, rows),
                (dq_ref, dq_hbm, rows),
                (dkv_own_ref, dkv_own_hbm, ext),
            ]
        ):
            results.append(
                pltpu.make_async_copy(source.at[at], target.at[at], sems.at[8 + 3 * i + k])
            )

    def lanes(column):
        bias = jnp.where(column.astype(f32) > 0.5, 0.0, NEG)
        return jnp.broadcast_to(bias, (bias.shape[0], 2 * tile))

    def outer(rows_ref):
        return jnp.dot(
            rows_ref[:, :width], wp_ref[:, width:], preferred_element_type=f32
        ).astype(bf16)

    kv_own_s[:halo] = outer(above_ref)
    kv_own_s[halo + tokens_dev :] = outer(below_ref)
    kv_aux_s[0] = outer(side_ref)
    tis_own_s[:halo] = lanes(above_ref[:, width : width + 1])
    tis_own_s[halo + tokens_dev :] = lanes(below_ref[:, width : width + 1])
    tis_side = lanes(side_ref[:, width : width + 1])

    lane = lax.broadcasted_iota(jnp.int32, (1, 2 * tile), 1) % tile
    query_row = lane // wide
    query_col = lane % wide

    row_base = lax.axis_index("row") * (bands * TILE_ROWS)
    col_base = lax.axis_index("col") * cols

    def window(key, query, base, extent):
        start = jnp.clip(base + query - RADIUS, 0, extent - KERNEL) - base
        return jnp.where((key >= start) & (key < start + KERNEL), 0.0, NEG)

    own_col = lax.broadcasted_iota(jnp.int32, (wide, 2 * tile), 0)
    aux_place = lax.broadcasted_iota(jnp.int32, (SIDE, 2 * tile), 0)
    far = -(2**20)
    first_col = jnp.where(aux_place < RADIUS, aux_place + wide, aux_place - 2 * RADIUS)
    first_col = jnp.where(aux_place < 2 * RADIUS, first_col, far)
    second_col = jnp.where(aux_place < RADIUS, aux_place + cols, aux_place + wide - SIDE)
    second_col = jnp.where(
        (aux_place < RADIUS) | (aux_place >= SIDE - RADIUS), second_col, far
    )
    for half, aux_col in enumerate((first_col, second_col)):
        shift = half * wide
        own_in = window(own_col + shift, query_col + shift, col_base, extents[1])
        aux_in = window(aux_col, query_col + shift, col_base, extents[1])
        own_same = jnp.where(own_col == query_col, 0.0, NEG)
        for key_row in range(KEY_ROWS):
            own_rows = slice(key_row * wide, (key_row + 1) * wide)
            aux_rows = slice(own_keys + key_row * SIDE, own_keys + (key_row + 1) * SIDE)
            for kind, first in enumerate((0, 2 * TILE_ROWS, (bands - 1) * TILE_ROWS)):
                row_in = window(key_row - RADIUS, query_row, row_base + first, extents[0])
                win_s[half, kind, own_rows] = own_in + row_in
                win_s[half, kind, aux_rows] = aux_in + row_in
            if half == 0:
                row_same = jnp.where(query_row == key_row - RADIUS, 0.0, NEG)
                self_s[own_rows] = own_same + row_same
                self_s[aux_rows] = jnp.full((SIDE, 2 * tile), NEG, f32)
    tissue = tissue_ref[...].astype(f32).T
    for index in range(bands):
        row = jnp.concatenate(
            [tissue[index * TILE_ROWS + k : index * TILE_ROWS + k + 1] for k in range(TILE_ROWS)],
            axis=1,
        )
        across = jnp.broadcast_to(row, (2 * tile, band)).T
        tis_own_s[halo + index * band : halo + (index + 1) * band] = jnp.where(
            across > 0.5, 0.0, NEG
        )
        for half in range(2):
            pieces = [
                tissue[
                    index * TILE_ROWS + row : index * TILE_ROWS + row + 1,
                    half * wide : (half + 1) * wide,
                ]
                for row in range(TILE_ROWS)
            ]
            gate_s[2 * index + half] = jnp.concatenate(pieces * 2, axis=1)

    place = lax.broadcasted_iota(jnp.int32, (rows_aux, 1), 0) % SIDE

    def parts(array, begin, count):
        across = array.shape[1]
        return array.reshape(rows_own // cols, cols, across)[:, begin : begin + count].reshape(
            -1, across
        )

    def with_inner(own, side):
        first = parts(own, wide, SIDE)
        second = parts(own, wide - SIDE, SIDE)
        return (
            jnp.where(place < RADIUS, first, side),
            jnp.where(place >= SIDE - RADIUS, second, side),
        )

    early[0].wait()
    tis_aux_s[0], tis_aux_s[1] = with_inner(tis_own_s[...], tis_side)
    two_rows = lax.broadcasted_iota(jnp.int32, (2 * SIDE, 1), 0) % SIDE

    def fill(index, carry):
        rows = pl.ds(pl.multiple_of(index * 2 * SIDE, 2 * SIDE), 2 * SIDE)
        side = kv_aux_s[0, rows, :].astype(f32)

        def inner(first):
            at = [
                pl.ds(pl.multiple_of(index * 2 * cols, 2 * cols) + row * cols + first, 2 * SIDE)
                for row in range(2)
            ]
            return [kv_own_s[place, :].astype(f32) for place in at]

        one = jnp.concatenate([block[:SIDE] for block in inner(wide)], axis=0)
        two = jnp.concatenate([block[SIDE:] for block in inner(wide - 2 * SIDE)], axis=0)
        kv_aux_s[0, rows, :] = jnp.where(two_rows < RADIUS, one, side).astype(bf16)
        kv_aux_s[1, rows, :] = jnp.where(two_rows >= SIDE - RADIUS, two, side).astype(bf16)
        return carry

    row_pairs = rows_aux // (2 * SIDE)
    ready = (part // cols + RADIUS) // 2
    lax.fori_loop(0, ready, fill, 0, unroll=4)
    seen_rows = KEY_ROWS - TILE_ROWS
    acc_own[: seen_rows * cols] = jnp.zeros((seen_rows * cols, 2 * width), f32)
    acc_aux[:, : seen_rows * SIDE] = jnp.zeros((2, seen_rows * SIDE, 2 * width), f32)
    pl_s[1][...] = jnp.zeros((keys_all, HEADS * tile), bf16)
    sg_s[1][...] = jnp.zeros((keys_all, HEADS * tile), bf16)
    for copy in early[1:3]:
        copy.wait()
    for copy in late:
        copy.start()

    def split(block):
        head = lax.broadcasted_iota(jnp.int32, block.shape, 1) // HEAD
        zero = jnp.zeros_like(block)
        return jnp.concatenate(
            [jnp.where(head == i, block, zero) for i in range(block.shape[1] // HEAD)], axis=0
        )

    def corner(one, two):
        zero = jnp.zeros_like(one)
        return jnp.concatenate(
            [jnp.concatenate([one, zero], axis=1), jnp.concatenate([zero, two], axis=1)], axis=0
        )

    def own_at(index, half, row):
        return pl.ds(pl.multiple_of(index * band, band) + row * cols + half * wide, wide)

    def aux_at(index, begin, count):
        step = TILE_ROWS * SIDE
        return pl.ds(pl.multiple_of(index * step, step) + begin * SIDE, count * SIDE)

    def queries(ref, index, half):
        return jnp.concatenate([ref[own_at(index, half, row), :] for row in range(TILE_ROWS)], axis=0)

    def key_rows(index, half, at):
        rows = [kv_own_s[own_at(index, half, row), at] for row in range(KEY_ROWS)]
        return jnp.concatenate(rows + [kv_aux_s[half, aux_at(index, 0, KEY_ROWS), at]], axis=0)

    def score_stage(index, half):
        kind = jnp.where(index == 0, 0, jnp.where(index == bands - 1, 2, 1))
        tis_keys = jnp.concatenate(
            [tis_own_s[own_at(index, half, row)] for row in range(KEY_ROWS)]
            + [tis_aux_s[half, aux_at(index, 0, KEY_ROWS)]],
            axis=0,
        )
        bias = jnp.maximum(tis_keys, self_s[...]) + win_s[half, kind]
        q, g = queries(q_ref, index, half), queries(g_ref, index, half)
        keys = key_rows(index, half, slice(0, width))
        values = key_rows(index, half, slice(width, 2 * width))
        product = functools.partial(
            lax.dot_general, dimension_numbers=dims(1, 1), preferred_element_type=f32
        )
        rest = product(
            jnp.concatenate([keys[:, most:], values[:, most:]], axis=1),
            corner(split(q[:, most:]), split(g[:, most:])),
        )
        cut = HEADS * tile - 4 * tile
        scores = jnp.concatenate(
            [product(keys[:, :most], split(q[:, :most])), rest[:, :cut]], axis=1
        )
        scores = scores + jnp.concatenate([bias] * PAIRS, axis=1)
        x_s[half][...] = scores
        top_s[half][...] = jnp.max(scores, axis=0, keepdims=True)
        dp_s[half][:, : 4 * tile] = product(values[:, :most], split(g[:, :most]))
        dp_s[half][:, 4 * tile :] = rest[:, cut:]

    def softmax_stage(index, half):
        top = top_s[half][...]
        total = jnp.zeros((8, HEADS * tile), f32)
        inner = jnp.zeros((8, HEADS * tile), f32)
        fold = lambda a: jnp.sum(a.reshape(CHUNK // 8, 8, HEADS * tile), axis=0)
        for begin in range(0, keys_all, CHUNK):
            at = slice(begin, begin + CHUNK)
            terms = jnp.exp(x_s[half][at] - top)
            x_s[half][at] = terms
            total = total + fold(terms)
            inner = inner + fold(terms * dp_s[half][at])
        inverse = 1.0 / jnp.sum(total, axis=0, keepdims=True)
        delta = jnp.sum(inner, axis=0, keepdims=True) * inverse
        weight = inverse * jnp.concatenate([gate_s[2 * index + half]] * PAIRS, axis=1)
        for begin in range(0, keys_all, CHUNK):
            at = slice(begin, begin + CHUNK)
            probs = x_s[half][at] * weight
            pl_s[half][at] = probs.astype(bf16)
            sg_s[half][at] = (probs * (dp_s[half][at] - delta)).astype(bf16)

    def product_stage(index, half):
        keys = key_rows(index, half, slice(0, width))
        values = key_rows(index, half, slice(width, 2 * width))
        probs_low = pl_s[half][...]
        score_grad = sg_s[half][...]
        first_head = lax.broadcasted_iota(jnp.int32, (tile, PAIR), 1) < HEAD
        for pair in range(PAIRS):
            at = slice(pair * PAIR, (pair + 1) * PAIR)
            for rows, weight, scale, out_ref in (
                (values, probs_low, 1.0, att_ref),
                (keys, score_grad, FACTOR, dq_ref),
            ):
                both = lax.dot_general(
                    rows[:, at], weight[:, at], dims(0, 0), preferred_element_type=f32
                ).T
                mixed = (jnp.where(first_head, both[:tile], both[tile:]) * scale).astype(bf16)
                for row in range(TILE_ROWS):
                    out_ref[own_at(index, half, row), at] = mixed[row * wide : (row + 1) * wide]
        q, g = queries(q_ref, index, half), queries(g_ref, index, half)
        rest = jnp.dot(
            jnp.concatenate([probs_low[:, 4 * tile :], score_grad[:, 4 * tile :]], axis=1),
            corner(split(g[:, most:]), split(q[:, most:])),
            preferred_element_type=f32,
        )
        cut = width - most
        dk = jnp.dot(score_grad[:, : 4 * tile], split(q[:, :most]), preferred_element_type=f32)
        dv = jnp.dot(probs_low[:, : 4 * tile], split(g[:, :most]), preferred_element_type=f32)
        for grad, at in (
            (dk, slice(0, most)),
            (rest[:, cut:], slice(most, width)),
            (dv, slice(width, width + most)),
            (rest[:, :cut], slice(width + most, 2 * width)),
        ):
            for row in range(KEY_ROWS):
                piece = grad[row * wide : (row + 1) * wide]
                if row < seen_rows:
                    acc_own[own_at(index, half, row), at] += piece
                else:
                    acc_own[own_at(index, half, row), at] = piece
            seen = own_keys + seen_rows * SIDE
            acc_aux[half, aux_at(index, 0, seen_rows), at] += grad[own_keys:seen]
            acc_aux[half, aux_at(index, seen_rows, TILE_ROWS), at] = grad[seen:]

    def merge(index, carry):
        rows = pl.ds(pl.multiple_of(index * 2 * SIDE, 2 * SIDE), 2 * SIDE)
        one, two = acc_aux[0, rows, :], acc_aux[1, rows, :]
        dkv_side_ref[rows, :] = jnp.where(
            two_rows < RADIUS, two, jnp.where(two_rows < 2 * RADIUS, one, 0.0)
        ).astype(bf16)
        one = jnp.where(two_rows < RADIUS, one, 0.0)
        two = jnp.where(two_rows >= SIDE - RADIUS, two, 0.0)
        for row in range(2):
            start = pl.multiple_of(index * 2 * cols, 2 * cols) + row * cols
            at = slice(row * SIDE, (row + 1) * SIDE)
            own = acc_own[pl.ds(start, cols), :]
            own = jnp.concatenate(
                [
                    own[: wide - SIDE],
                    own[wide - SIDE : wide] + two[at],
                    own[wide : wide + SIDE] + one[at],
                    own[wide + SIDE :],
                ],
                axis=0,
            )
            dkv_own_ref[pl.ds(start, cols), :] = own.astype(bf16)
        return carry

    final = done // (2 * cols)
    more_keys = (part // cols - TILE_ROWS - RADIUS) // (TILE_ROWS * SPAN)
    first_done = bands // 2 // SPAN + 1
    score_stage(0, 0)

    def step(group, carry):
        @pl.when(group == more_keys)
        def _():
            for copy in early[3:]:
                copy.wait()
            lax.fori_loop(ready, row_pairs, fill, 0, unroll=4)

        @pl.when(group == first_done)
        def _():
            lax.fori_loop(0, final, merge, 0, unroll=4)
            for copy in results[:3]:
                copy.start()

        for slot in range(2 * SPAN):
            index = group * SPAN + slot // 2
            half = slot % 2
            if half == 0:
                product_stage(jnp.maximum(index - 1, 0), 1)
            else:
                product_stage(index, 0)
            softmax_stage(index, half)
            if half == 0:
                score_stage(index, 1)
            else:
                score_stage(jnp.minimum(index + 1, bands - 1), 0)
        return carry

    lax.fori_loop(0, bands // SPAN, step, 0)
    product_stage(bands - 1, 1)

    lax.fori_loop(final, row_pairs, merge, 0, unroll=4)
    for copy in results[3:]:
        copy.start()
    for copy in late:
        copy.wait()
    send_row = lax.broadcasted_iota(jnp.int32, (128, 256), 0)
    side_row = lax.broadcasted_iota(jnp.int32, (128, 256), 1)
    place = (send_row // (SIDE // 2)) * SIDE + send_row % (SIDE // 2)
    for begin, send_ref in ((RADIUS, to_left_ref), (0, to_right_ref)):
        pick = jnp.where(side_row == place + begin, 1.0, 0.0).astype(bf16)
        for first in range(0, send_ref.shape[0], 128):
            count = min(128, send_ref.shape[0] - first)
            source = dkv_side_ref[2 * first : min(2 * (first + count), dkv_side_ref.shape[0])]
            send_ref[first : first + count] = jnp.dot(
                pick[:count, : source.shape[0]], source, preferred_element_type=f32
            ).astype(bf16)
    outside = jnp.concatenate(
        [above_ref[:, :width], below_ref[:, :width], side_ref[:, :width]], axis=0
    )

    def put(block, value):
        value = value.astype(bf16)
        for i in range(value.shape[1] // 128):
            part_ref[(block + i) * width : (block + i + 1) * width] = value[
                :, i * 128 : (i + 1) * 128
            ]

    columns = width // 128
    put(0, jnp.dot(tok_t_ref[...], dq_ref[...], preferred_element_type=f32))
    for begin in range(0, 2 * width, 256):
        at = slice(begin, begin + 256)
        grad_outside = jnp.concatenate(
            [dkv_own_ref[:halo, at], dkv_own_ref[halo + tokens_dev :, at], dkv_side_ref[:, at]],
            axis=0,
        )
        put(
            columns + begin // 128,
            jnp.dot(
                tok_t_ref[...],
                dkv_own_ref[halo : halo + tokens_dev, at],
                preferred_element_type=f32,
            )
            + lax.dot_general(outside, grad_outside, dims(0, 0), preferred_element_type=f32),
        )
    put(3 * columns, lax.dot_general(
            att_ref[...], cot_ref[...], dims(0, 0), preferred_element_type=f32
        ))
    used = 4 * width * columns
    if used < part_ref.shape[0]:
        part_ref[used:] = jnp.zeros((part_ref.shape[0] - used, 128), bf16)
    for copy in results:
        copy.wait()


def attention(
    above, below, side, q, kv, g, tok_t, cot, wp, tissue, extents, rows_part
):
    tokens_dev, width = cot.shape
    rows_own = tokens_dev + 2 * above.shape[0]
    rows_side = side.shape[0]
    cols = tissue.shape[0]
    tile = TILE_ROWS * cols // 2
    keys_all = KEY_ROWS * (cols // 2 + SIDE)
    rows_send = -(-rows_side // 32) * 16
    vmem = pl.BlockSpec(memory_space=pltpu.VMEM)
    hbm = pl.BlockSpec(memory_space=pl.ANY)
    stage = []
    for shape, kind in (
        ((keys_all, HEADS * tile), f32),
        ((keys_all, HEADS * tile), f32),
        ((1, HEADS * tile), f32),
        ((keys_all, HEADS * tile), bf16),
        ((keys_all, HEADS * tile), bf16),
    ):
        stage += [pltpu.VMEM(shape, kind)] * 2
    return pl.pallas_call(
        functools.partial(attention_kernel, extents),
        out_shape=[
            jax.ShapeDtypeStruct((tokens_dev, width), bf16),
            jax.ShapeDtypeStruct((tokens_dev, width), bf16),
            jax.ShapeDtypeStruct((rows_own, 2 * width), bf16),
            jax.ShapeDtypeStruct((rows_send, 2 * width), bf16),
            jax.ShapeDtypeStruct((rows_send, 2 * width), bf16),
            jax.ShapeDtypeStruct((rows_part, 128), bf16),
        ],
        in_specs=[vmem] * 3 + [hbm] * 5 + [vmem] * 2,
        out_specs=[hbm] * 3 + [vmem] * 3,
        scratch_shapes=[
            pltpu.VMEM((tokens_dev, width), bf16),
            pltpu.VMEM((tokens_dev, width), bf16),
            pltpu.VMEM((tokens_dev, width), bf16),
            pltpu.VMEM((width, tokens_dev), bf16),
            pltpu.VMEM((tokens_dev, width), bf16),
            pltpu.VMEM((tokens_dev, width), bf16),
            pltpu.VMEM((rows_own, 2 * width), bf16),
            pltpu.VMEM((rows_side, 2 * width), bf16),
            pltpu.VMEM((rows_own, 2 * width), bf16),
            pltpu.VMEM((2, rows_side, 2 * width), bf16),
            pltpu.VMEM((rows_own, 2 * tile), f32),
            pltpu.VMEM((2, rows_side, 2 * tile), f32),
            pltpu.VMEM((2, 3, keys_all, 2 * tile), f32),
            pltpu.VMEM((keys_all, 2 * tile), f32),
            pltpu.VMEM((2 * tokens_dev // (2 * tile), 1, 2 * tile), f32),
            pltpu.VMEM((rows_own, 2 * width), f32),
            pltpu.VMEM((2, rows_side, 2 * width), f32),
            pltpu.SemaphoreType.DMA((14,)),
        ]
        + stage,
        compiler_params=pltpu.CompilerParams(vmem_limit_bytes=56 * MIB),
        name="attention",
    )(above, below, side, q, kv, g, tok_t, cot, wp, tissue)


def to_next(array, axis):
    count = lax.axis_size(axis)
    return lax.ppermute(array, axis, [(i, (i + 1) % count) for i in range(count)])


def to_last(array, axis):
    count = lax.axis_size(axis)
    return lax.ppermute(array, axis, [((i + 1) % count, i) for i in range(count)])


def sum_kernel(pieces, pieces_ref, copies_ref):
    rows = pieces_ref.shape[0] // pieces
    pair = 2 * rows
    total = jnp.zeros((pair, 128), f32)
    for i in range(pieces // 2):
        total = total + pieces_ref[i * pair : (i + 1) * pair].astype(f32)
    total = total[:rows] + total[rows:]
    total = jnp.concatenate([total, total], axis=0).astype(bf16)
    for i in range(pieces // 2):
        copies_ref[i * pair : (i + 1) * pair] = total


def summed_copies(pieces, count):
    return pl.pallas_call(
        functools.partial(sum_kernel, count),
        out_shape=jax.ShapeDtypeStruct(pieces.shape, bf16),
        compiler_params=pltpu.CompilerParams(vmem_limit_bytes=16 * MIB),
        name="summed_copies",
    )(pieces)


def total_over_devices(partial):
    axes = ("row", "col")
    count = lax.axis_size("row") * lax.axis_size("col")
    pieces = lax.all_to_all(partial.reshape(count, -1, 128), axes, 0, 0, tiled=True)
    copies = summed_copies(pieces.reshape(partial.shape), count).reshape(pieces.shape)
    return lax.all_to_all(copies, axes, 0, 0, tiled=True).reshape(partial.shape)


def unpack_kernel(scale, whole_ref, packed_ref, output_ref):
    width = output_ref.shape[0]
    for block in range((packed_ref.shape[1] + output_ref.shape[1]) // 128):
        value = whole_ref[block * width : (block + 1) * width].astype(f32) * scale
        column = block * 128
        if column < packed_ref.shape[1]:
            packed_ref[:, column : column + 128] = value
        else:
            column -= packed_ref.shape[1]
            output_ref[:, column : column + 128] = value


def unpack(whole, width, scale):
    return pl.pallas_call(
        functools.partial(unpack_kernel, scale),
        out_shape=[
            jax.ShapeDtypeStruct((width, 3 * width), f32),
            jax.ShapeDtypeStruct((width, width), f32),
        ],
        compiler_params=pltpu.CompilerParams(vmem_limit_bytes=24 * MIB),
        name="unpack",
    )(whole)


def per_device(tokens, tissue, cotangent, packed_weight, output_weight):
    rows_dev, cols_dev, width = tokens.shape
    ext_rows = rows_dev + 2 * RADIUS
    devices = lax.axis_size("row") * lax.axis_size("col")
    rows_part = -(-4 * width * (width // 128) // (8 * devices)) * 8 * devices
    total_scale = float(rows_dev * lax.axis_size("row") * cols_dev * lax.axis_size("col")) ** (-0.5)
    token_rows = tokens.reshape(-1, width)
    cotangent_rows = cotangent.reshape(-1, width)

    with_tissue = lambda a, b: jnp.concatenate([a, b.astype(bf16)[..., None]], axis=-1)
    above = to_next(with_tissue(tokens[-RADIUS:], tissue[-RADIUS:]), "row")
    below = to_last(with_tissue(tokens[:RADIUS], tissue[:RADIUS]), "row")
    left_cols = with_tissue(tokens[:, :RADIUS], tissue[:, :RADIUS])
    right_cols = with_tissue(tokens[:, -RADIUS:], tissue[:, -RADIUS:])
    left_cols = jnp.concatenate([above[:, :RADIUS], left_cols, below[:, :RADIUS]], axis=0)
    right_cols = jnp.concatenate([above[:, -RADIUS:], right_cols, below[:, -RADIUS:]], axis=0)
    from_left = to_next(right_cols, "col")
    from_right = to_last(left_cols, "col")
    pad = jnp.zeros((ext_rows, SIDE - 2 * RADIUS, width + 1), bf16)
    side = jnp.concatenate([from_right, from_left, pad], axis=1).reshape(-1, width + 1)

    q, kv, g, tok_t = project(token_rows, cotangent_rows, packed_weight, output_weight)
    attended, dq, dkv_own, to_left, to_right, partial = attention(
        above.reshape(-1, width + 1), below.reshape(-1, width + 1), side,
        q, kv, g, tok_t, cotangent_rows, packed_weight, tissue.T,
        (rows_dev * lax.axis_size("row"), cols_dev * lax.axis_size("col")), rows_part,
    )

    half = SIDE // 2

    def columns(sent):
        return sent[: ext_rows * half].reshape(ext_rows, half, 2 * width)[:, :RADIUS]

    from_right = columns(to_last(to_left, "col"))
    from_left = columns(to_next(to_right, "col"))
    dkv_own = dkv_own.reshape(ext_rows, cols_dev, 2 * width)
    first, last, inner = slice(None, RADIUS), slice(-RADIUS, None), slice(RADIUS, -RADIUS)

    def with_columns(rows):
        between = jnp.zeros((dkv_own[rows].shape[0], cols_dev - 2 * RADIUS, 2 * width), bf16)
        beside = jnp.concatenate([from_left[rows], between, from_right[rows]], axis=1)
        return dkv_own[rows].astype(f32) + beside.astype(f32)

    from_below = to_last(with_columns(first).astype(bf16), "row")
    from_above = to_next(with_columns(last).astype(bf16), "row")
    between = jnp.zeros((rows_dev - 2 * RADIUS, cols_dev, 2 * width), bf16)
    beside = jnp.concatenate([from_above, between, from_below], axis=0)
    dkv = with_columns(inner) + beside.astype(f32)
    dkv = dkv.astype(bf16).reshape(-1, 2 * width)

    contract = functools.partial(lax.dot_general, preferred_element_type=f32)
    layer_out = (
        token_rows.astype(f32) + jnp.dot(attended, output_weight, preferred_element_type=f32)
    ).astype(bf16)
    grad_tokens = (
        cotangent_rows.astype(f32)
        + contract(dq, packed_weight[:, :width], dims(1, 1))
        + contract(dkv, packed_weight[:, width:], dims(1, 1))
    ).astype(bf16)
    grad_packed, grad_output = unpack(total_over_devices(partial), width, total_scale)
    return (
        layer_out.reshape(rows_dev, cols_dev, width),
        grad_tokens.reshape(rows_dev, cols_dev, width),
        grad_packed,
        grad_output,
    )


def solution(mesh):
    in_specs = (P("row", "col", None), P("row", "col"), P("row", "col", None), P(), P())
    out_specs = (P("row", "col", None), P("row", "col", None), P(), P())
    return jax.shard_map(
        per_device, mesh=mesh, in_specs=in_specs, out_specs=out_specs, check_vma=False
    )
```

```python
import functools

import jax
import jax.numpy as jnp
from jax import lax
from jax.experimental import pallas as pl
from jax.experimental.pallas import tpu as pltpu
from jax.sharding import PartitionSpec as P

HEADS = 6
HEAD = 64
KERNEL = 7
RADIUS = 3
PAIR = 2 * HEAD
PAIRS = HEADS // 2
SIDE = 8
TILE_ROWS = 4
KEY_ROWS = TILE_ROWS + 2 * RADIUS
CHUNK = 48
SPAN = 4
PROJECT_STEPS = 2
FACTOR = HEAD ** (-0.5)
NEG = float("-inf")
MIB = 1024 * 1024
f32 = jnp.float32
bf16 = jnp.bfloat16


def dims(lhs, rhs):
    return (((lhs,), (rhs,)), ((), ()))


def project_kernel(
    tok_ref, cot_ref, wp_ref, wo_ref, q_ref, kv_ref, g_ref, tok_t_ref
):
    width = tok_ref.shape[1]
    tok = tok_ref[...]
    q = jnp.dot(tok, wp_ref[:, :width], preferred_element_type=f32).astype(bf16)
    q_ref[...] = (q * FACTOR).astype(bf16)
    kv_ref[...] = jnp.dot(tok, wp_ref[:, width:], preferred_element_type=f32).astype(bf16)
    g_ref[...] = lax.dot_general(
        cot_ref[...], wo_ref[...], dims(1, 1), preferred_element_type=f32
    ).astype(bf16)
    tok_t_ref[...] = tok.T


def project(tok, cot, wp, wo):
    count, width = tok.shape
    rows = count // PROJECT_STEPS
    block = lambda cols: pl.BlockSpec((rows, cols), lambda i: (i, 0))
    whole = lambda a: pl.BlockSpec(a.shape, lambda i: (0, 0))
    return pl.pallas_call(
        project_kernel,
        grid=(count // rows,),
        out_shape=[
            jax.ShapeDtypeStruct((count, width), bf16),
            jax.ShapeDtypeStruct((count, 2 * width), bf16),
            jax.ShapeDtypeStruct((count, width), bf16),
            jax.ShapeDtypeStruct((width, count), bf16),
        ],
        in_specs=[block(width), block(width), whole(wp), whole(wo)],
        out_specs=[
            block(width),
            block(2 * width),
            block(width),
            pl.BlockSpec((width, rows), lambda i: (0, i)),
        ],
        compiler_params=pltpu.CompilerParams(vmem_limit_bytes=56 * MIB),
        cost_estimate=pl.CostEstimate(
            flops=2 * count * width * 4 * width, bytes_accessed=14 * count * width, transcendentals=0
        ),
        name="project",
    )(tok, cot, wp, wo)


def attention_kernel(
    extents,
    above_ref, below_ref, side_ref, q_hbm, kv_hbm, g_hbm, tok_t_hbm, cot_hbm, wp_ref, tissue_ref,
    att_hbm, dq_hbm, dkv_own_hbm, to_left_ref, to_right_ref, part_ref,
    cot_ref, q_ref, g_ref, tok_t_ref, att_ref, dq_ref, dkv_own_ref, dkv_side_ref,
    kv_own_s, kv_aux_s, tis_own_s, tis_aux_s, win_s, self_s, gate_s, acc_own, acc_aux, sems, *stage,
):
    tokens_dev, width = q_ref.shape
    halo = above_ref.shape[0]
    rows_own = tokens_dev + 2 * halo
    rows_aux = side_ref.shape[0]
    cols = halo // RADIUS
    wide = cols // 2
    tile = TILE_ROWS * wide
    band = TILE_ROWS * cols
    bands = tokens_dev // band
    own_keys = KEY_ROWS * wide
    aux_keys = KEY_ROWS * SIDE
    keys_all = own_keys + aux_keys
    most = 4 * HEAD
    x_s, dp_s, top_s, pl_s, sg_s = (stage[2 * i : 2 * i + 2] for i in range(5))

    part = tokens_dev // 2
    early = []
    for i in range(2):
        rows = pl.ds(i * part, part)
        targets = (kv_own_s.at[pl.ds(halo + i * part, part)], q_ref.at[rows], g_ref.at[rows])
        for k, (source, target) in enumerate(zip((kv_hbm, q_hbm, g_hbm), targets)):
            early.append(pltpu.make_async_copy(source.at[rows], target, sems.at[3 * i + k]))
    for copy in early:
        copy.start()
    late = [
        pltpu.make_async_copy(tok_t_hbm, tok_t_ref, sems.at[6]),
        pltpu.make_async_copy(cot_hbm, cot_ref, sems.at[7]),
    ]
    done = tokens_dev // 2
    results = []
    for i in range(2):
        rows = pl.ds(i * done, done)
        ext = rows if i == 0 else pl.ds(done, rows_own - done)
        for k, (source, target, at) in enumerate(
            [
                (att_ref, att_hbm, rows),
                (dq_ref, dq_hbm, rows),
                (dkv_own_ref, dkv_own_hbm, ext),
            ]
        ):
            results.append(
                pltpu.make_async_copy(source.at[at], target.at[at], sems.at[8 + 3 * i + k])
            )

    def lanes(column):
        bias = jnp.where(column.astype(f32) > 0.5, 0.0, NEG)
        return jnp.broadcast_to(bias, (bias.shape[0], 2 * tile))

    def outer(rows_ref):
        return jnp.dot(
            rows_ref[:, :width], wp_ref[:, width:], preferred_element_type=f32
        ).astype(bf16)

    kv_own_s[:halo] = outer(above_ref)
    kv_own_s[halo + tokens_dev :] = outer(below_ref)
    kv_aux_s[0] = outer(side_ref)
    tis_own_s[:halo] = lanes(above_ref[:, width : width + 1])
    tis_own_s[halo + tokens_dev :] = lanes(below_ref[:, width : width + 1])
    tis_side = lanes(side_ref[:, width : width + 1])

    lane = lax.broadcasted_iota(jnp.int32, (1, 2 * tile), 1) % tile
    query_row = lane // wide
    query_col = lane % wide

    row_base = lax.axis_index("row") * (bands * TILE_ROWS)
    col_base = lax.axis_index("col") * cols

    def window(key, query, base, extent):
        start = jnp.clip(base + query - RADIUS, 0, extent - KERNEL) - base
        return jnp.where((key >= start) & (key < start + KERNEL), 0.0, NEG)

    own_col = lax.broadcasted_iota(jnp.int32, (wide, 2 * tile), 0)
    aux_place = lax.broadcasted_iota(jnp.int32, (SIDE, 2 * tile), 0)
    far = -(2**20)
    first_col = jnp.where(aux_place < RADIUS, aux_place + wide, aux_place - 2 * RADIUS)
    first_col = jnp.where(aux_place < 2 * RADIUS, first_col, far)
    second_col = jnp.where(aux_place < RADIUS, aux_place + cols, aux_place + wide - SIDE)
    second_col = jnp.where(
        (aux_place < RADIUS) | (aux_place >= SIDE - RADIUS), second_col, far
    )
    for half, aux_col in enumerate((first_col, second_col)):
        shift = half * wide
        own_in = window(own_col + shift, query_col + shift, col_base, extents[1])
        aux_in = window(aux_col, query_col + shift, col_base, extents[1])
        own_same = jnp.where(own_col == query_col, 0.0, NEG)
        for key_row in range(KEY_ROWS):
            own_rows = slice(key_row * wide, (key_row + 1) * wide)
            aux_rows = slice(own_keys + key_row * SIDE, own_keys + (key_row + 1) * SIDE)
            for kind, first in enumerate((0, 2 * TILE_ROWS, (bands - 1) * TILE_ROWS)):
                row_in = window(key_row - RADIUS, query_row, row_base + first, extents[0])
                win_s[half, kind, own_rows] = own_in + row_in
                win_s[half, kind, aux_rows] = aux_in + row_in
            if half == 0:
                row_same = jnp.where(query_row == key_row - RADIUS, 0.0, NEG)
                self_s[own_rows] = own_same + row_same
                self_s[aux_rows] = jnp.full((SIDE, 2 * tile), NEG, f32)
    tissue = tissue_ref[...].astype(f32).T
    for index in range(bands):
        row = jnp.concatenate(
            [tissue[index * TILE_ROWS + k : index * TILE_ROWS + k + 1] for k in range(TILE_ROWS)],
            axis=1,
        )
        across = jnp.broadcast_to(row, (2 * tile, band)).T
        tis_own_s[halo + index * band : halo + (index + 1) * band] = jnp.where(
            across > 0.5, 0.0, NEG
        )
        for half in range(2):
            pieces = [
                tissue[
                    index * TILE_ROWS + row : index * TILE_ROWS + row + 1,
                    half * wide : (half + 1) * wide,
                ]
                for row in range(TILE_ROWS)
            ]
            gate_s[2 * index + half] = jnp.concatenate(pieces * 2, axis=1)

    place = lax.broadcasted_iota(jnp.int32, (rows_aux, 1), 0) % SIDE

    def parts(array, begin, count):
        across = array.shape[1]
        return array.reshape(rows_own // cols, cols, across)[:, begin : begin + count].reshape(
            -1, across
        )

    def with_inner(own, side):
        first = parts(own, wide, SIDE)
        second = parts(own, wide - SIDE, SIDE)
        return (
            jnp.where(place < RADIUS, first, side),
            jnp.where(place >= SIDE - RADIUS, second, side),
        )

    early[0].wait()
    tis_aux_s[0], tis_aux_s[1] = with_inner(tis_own_s[...], tis_side)
    two_rows = lax.broadcasted_iota(jnp.int32, (2 * SIDE, 1), 0) % SIDE

    def fill(index, carry):
        rows = pl.ds(pl.multiple_of(index * 2 * SIDE, 2 * SIDE), 2 * SIDE)
        side = kv_aux_s[0, rows, :].astype(f32)

        def inner(first):
            at = [
                pl.ds(pl.multiple_of(index * 2 * cols, 2 * cols) + row * cols + first, 2 * SIDE)
                for row in range(2)
            ]
            return [kv_own_s[place, :].astype(f32) for place in at]

        one = jnp.concatenate([block[:SIDE] for block in inner(wide)], axis=0)
        two = jnp.concatenate([block[SIDE:] for block in inner(wide - 2 * SIDE)], axis=0)
        kv_aux_s[0, rows, :] = jnp.where(two_rows < RADIUS, one, side).astype(bf16)
        kv_aux_s[1, rows, :] = jnp.where(two_rows >= SIDE - RADIUS, two, side).astype(bf16)
        return carry

    row_pairs = rows_aux // (2 * SIDE)
    ready = (part // cols + RADIUS) // 2
    lax.fori_loop(0, ready, fill, 0, unroll=4)
    seen_rows = KEY_ROWS - TILE_ROWS
    acc_own[: seen_rows * cols] = jnp.zeros((seen_rows * cols, 2 * width), f32)
    acc_aux[:, : seen_rows * SIDE] = jnp.zeros((2, seen_rows * SIDE, 2 * width), f32)
    pl_s[1][...] = jnp.zeros((keys_all, HEADS * tile), bf16)
    sg_s[1][...] = jnp.zeros((keys_all, HEADS * tile), bf16)
    for copy in early[1:3]:
        copy.wait()
    for copy in late:
        copy.start()

    def split(block):
        head = lax.broadcasted_iota(jnp.int32, block.shape, 1) // HEAD
        zero = jnp.zeros_like(block)
        return jnp.concatenate(
            [jnp.where(head == i, block, zero) for i in range(block.shape[1] // HEAD)], axis=0
        )

    def corner(one, two):
        zero = jnp.zeros_like(one)
        return jnp.concatenate(
            [jnp.concatenate([one, zero], axis=1), jnp.concatenate([zero, two], axis=1)], axis=0
        )

    def own_at(index, half, row):
        return pl.ds(pl.multiple_of(index * band, band) + row * cols + half * wide, wide)

    def aux_at(index, begin, count):
        step = TILE_ROWS * SIDE
        return pl.ds(pl.multiple_of(index * step, step) + begin * SIDE, count * SIDE)

    def queries(ref, index, half):
        return jnp.concatenate([ref[own_at(index, half, row), :] for row in range(TILE_ROWS)], axis=0)

    def key_rows(index, half, at):
        rows = [kv_own_s[own_at(index, half, row), at] for row in range(KEY_ROWS)]
        return jnp.concatenate(rows + [kv_aux_s[half, aux_at(index, 0, KEY_ROWS), at]], axis=0)

    def score_stage(index, half):
        kind = jnp.where(index == 0, 0, jnp.where(index == bands - 1, 2, 1))
        tis_keys = jnp.concatenate(
            [tis_own_s[own_at(index, half, row)] for row in range(KEY_ROWS)]
            + [tis_aux_s[half, aux_at(index, 0, KEY_ROWS)]],
            axis=0,
        )
        bias = jnp.maximum(tis_keys, self_s[...]) + win_s[half, kind]
        q, g = queries(q_ref, index, half), queries(g_ref, index, half)
        keys = key_rows(index, half, slice(0, width))
        values = key_rows(index, half, slice(width, 2 * width))
        product = functools.partial(
            lax.dot_general, dimension_numbers=dims(1, 1), preferred_element_type=f32
        )
        rest = product(
            jnp.concatenate([keys[:, most:], values[:, most:]], axis=1),
            corner(split(q[:, most:]), split(g[:, most:])),
        )
        cut = HEADS * tile - 4 * tile
        scores = jnp.concatenate(
            [product(keys[:, :most], split(q[:, :most])), rest[:, :cut]], axis=1
        )
        scores = scores + jnp.concatenate([bias] * PAIRS, axis=1)
        x_s[half][...] = scores
        top_s[half][...] = jnp.max(scores, axis=0, keepdims=True)
        dp_s[half][:, : 4 * tile] = product(values[:, :most], split(g[:, :most]))
        dp_s[half][:, 4 * tile :] = rest[:, cut:]

    def softmax_stage(index, half):
        top = top_s[half][...]
        total = jnp.zeros((8, HEADS * tile), f32)
        inner = jnp.zeros((8, HEADS * tile), f32)
        fold = lambda a: jnp.sum(a.reshape(CHUNK // 8, 8, HEADS * tile), axis=0)
        for begin in range(0, keys_all, CHUNK):
            at = slice(begin, begin + CHUNK)
            terms = jnp.exp(x_s[half][at] - top)
            x_s[half][at] = terms
            total = total + fold(terms)
            inner = inner + fold(terms * dp_s[half][at])
        inverse = 1.0 / jnp.sum(total, axis=0, keepdims=True)
        delta = jnp.sum(inner, axis=0, keepdims=True) * inverse
        weight = inverse * jnp.concatenate([gate_s[2 * index + half]] * PAIRS, axis=1)
        for begin in range(0, keys_all, CHUNK):
            at = slice(begin, begin + CHUNK)
            probs = x_s[half][at] * weight
            pl_s[half][at] = probs.astype(bf16)
            sg_s[half][at] = (probs * (dp_s[half][at] - delta)).astype(bf16)

    def product_stage(index, half):
        keys = key_rows(index, half, slice(0, width))
        values = key_rows(index, half, slice(width, 2 * width))
        probs_low = pl_s[half][...]
        score_grad = sg_s[half][...]
        first_head = lax.broadcasted_iota(jnp.int32, (tile, PAIR), 1) < HEAD
        for pair in range(PAIRS):
            at = slice(pair * PAIR, (pair + 1) * PAIR)
            for rows, weight, scale, out_ref in (
                (values, probs_low, 1.0, att_ref),
                (keys, score_grad, FACTOR, dq_ref),
            ):
                both = lax.dot_general(
                    rows[:, at], weight[:, at], dims(0, 0), preferred_element_type=f32
                ).T
                mixed = (jnp.where(first_head, both[:tile], both[tile:]) * scale).astype(bf16)
                for row in range(TILE_ROWS):
                    out_ref[own_at(index, half, row), at] = mixed[row * wide : (row + 1) * wide]
        q, g = queries(q_ref, index, half), queries(g_ref, index, half)
        rest = jnp.dot(
            jnp.concatenate([probs_low[:, 4 * tile :], score_grad[:, 4 * tile :]], axis=1),
            corner(split(g[:, most:]), split(q[:, most:])),
            preferred_element_type=f32,
        )
        cut = width - most
        dk = jnp.dot(score_grad[:, : 4 * tile], split(q[:, :most]), preferred_element_type=f32)
        dv = jnp.dot(probs_low[:, : 4 * tile], split(g[:, :most]), preferred_element_type=f32)
        for grad, at in (
            (dk, slice(0, most)),
            (rest[:, cut:], slice(most, width)),
            (dv, slice(width, width + most)),
            (rest[:, :cut], slice(width + most, 2 * width)),
        ):
            for row in range(KEY_ROWS):
                piece = grad[row * wide : (row + 1) * wide]
                if row < seen_rows:
                    acc_own[own_at(index, half, row), at] += piece
                else:
                    acc_own[own_at(index, half, row), at] = piece
            seen = own_keys + seen_rows * SIDE
            acc_aux[half, aux_at(index, 0, seen_rows), at] += grad[own_keys:seen]
            acc_aux[half, aux_at(index, seen_rows, TILE_ROWS), at] = grad[seen:]

    def merge(index, carry):
        rows = pl.ds(pl.multiple_of(index * 2 * SIDE, 2 * SIDE), 2 * SIDE)
        one, two = acc_aux[0, rows, :], acc_aux[1, rows, :]
        dkv_side_ref[rows, :] = jnp.where(
            two_rows < RADIUS, two, jnp.where(two_rows < 2 * RADIUS, one, 0.0)
        ).astype(bf16)
        one = jnp.where(two_rows < RADIUS, one, 0.0)
        two = jnp.where(two_rows >= SIDE - RADIUS, two, 0.0)
        for row in range(2):
            start = pl.multiple_of(index * 2 * cols, 2 * cols) + row * cols
            at = slice(row * SIDE, (row + 1) * SIDE)
            own = acc_own[pl.ds(start, cols), :]
            own = jnp.concatenate(
                [
                    own[: wide - SIDE],
                    own[wide - SIDE : wide] + two[at],
                    own[wide : wide + SIDE] + one[at],
                    own[wide + SIDE :],
                ],
                axis=0,
            )
            dkv_own_ref[pl.ds(start, cols), :] = own.astype(bf16)
        return carry

    final = done // (2 * cols)
    more_keys = (part // cols - TILE_ROWS - RADIUS) // (TILE_ROWS * SPAN)
    first_done = bands // 2 // SPAN + 1
    score_stage(0, 0)

    def step(group, carry):
        @pl.when(group == more_keys)
        def _():
            for copy in early[3:]:
                copy.wait()
            lax.fori_loop(ready, row_pairs, fill, 0, unroll=4)

        @pl.when(group == first_done)
        def _():
            lax.fori_loop(0, final, merge, 0, unroll=4)
            for copy in results[:3]:
                copy.start()

        for slot in range(2 * SPAN):
            index = group * SPAN + slot // 2
            half = slot % 2
            if half == 0:
                product_stage(jnp.maximum(index - 1, 0), 1)
            else:
                product_stage(index, 0)
            softmax_stage(index, half)
            if half == 0:
                score_stage(index, 1)
            else:
                score_stage(jnp.minimum(index + 1, bands - 1), 0)
        return carry

    lax.fori_loop(0, bands // SPAN, step, 0)
    product_stage(bands - 1, 1)

    lax.fori_loop(final, row_pairs, merge, 0, unroll=4)
    for copy in results[3:]:
        copy.start()
    for copy in late:
        copy.wait()
    send_row = lax.broadcasted_iota(jnp.int32, (128, 256), 0)
    side_row = lax.broadcasted_iota(jnp.int32, (128, 256), 1)
    place = (send_row // (SIDE // 2)) * SIDE + send_row % (SIDE // 2)
    for begin, send_ref in ((RADIUS, to_left_ref), (0, to_right_ref)):
        pick = jnp.where(side_row == place + begin, 1.0, 0.0).astype(bf16)
        for first in range(0, send_ref.shape[0], 128):
            count = min(128, send_ref.shape[0] - first)
            source = dkv_side_ref[2 * first : min(2 * (first + count), dkv_side_ref.shape[0])]
            send_ref[first : first + count] = jnp.dot(
                pick[:count, : source.shape[0]], source, preferred_element_type=f32
            ).astype(bf16)
    outside = jnp.concatenate(
        [above_ref[:, :width], below_ref[:, :width], side_ref[:, :width]], axis=0
    )

    def put(block, value):
        value = value.astype(bf16)
        for i in range(value.shape[1] // 128):
            part_ref[(block + i) * width : (block + i + 1) * width] = value[
                :, i * 128 : (i + 1) * 128
            ]

    columns = width // 128
    put(0, jnp.dot(tok_t_ref[...], dq_ref[...], preferred_element_type=f32))
    for begin in range(0, 2 * width, 256):
        at = slice(begin, begin + 256)
        grad_outside = jnp.concatenate(
            [dkv_own_ref[:halo, at], dkv_own_ref[halo + tokens_dev :, at], dkv_side_ref[:, at]],
            axis=0,
        )
        put(
            columns + begin // 128,
            jnp.dot(
                tok_t_ref[...],
                dkv_own_ref[halo : halo + tokens_dev, at],
                preferred_element_type=f32,
            )
            + lax.dot_general(outside, grad_outside, dims(0, 0), preferred_element_type=f32),
        )
    put(3 * columns, lax.dot_general(
            att_ref[...], cot_ref[...], dims(0, 0), preferred_element_type=f32
        ))
    used = 4 * width * columns
    if used < part_ref.shape[0]:
        part_ref[used:] = jnp.zeros((part_ref.shape[0] - used, 128), bf16)
    for copy in results:
        copy.wait()


def attention(
    above, below, side, q, kv, g, tok_t, cot, wp, tissue, extents, rows_part
):
    tokens_dev, width = cot.shape
    rows_own = tokens_dev + 2 * above.shape[0]
    rows_side = side.shape[0]
    cols = tissue.shape[0]
    tile = TILE_ROWS * cols // 2
    keys_all = KEY_ROWS * (cols // 2 + SIDE)
    rows_send = -(-rows_side // 32) * 16
    vmem = pl.BlockSpec(memory_space=pltpu.VMEM)
    hbm = pl.BlockSpec(memory_space=pl.ANY)
    stage = []
    for shape, kind in (
        ((keys_all, HEADS * tile), f32),
        ((keys_all, HEADS * tile), f32),
        ((1, HEADS * tile), f32),
        ((keys_all, HEADS * tile), bf16),
        ((keys_all, HEADS * tile), bf16),
    ):
        stage += [pltpu.VMEM(shape, kind)] * 2
    return pl.pallas_call(
        functools.partial(attention_kernel, extents),
        out_shape=[
            jax.ShapeDtypeStruct((tokens_dev, width), bf16),
            jax.ShapeDtypeStruct((tokens_dev, width), bf16),
            jax.ShapeDtypeStruct((rows_own, 2 * width), bf16),
            jax.ShapeDtypeStruct((rows_send, 2 * width), bf16),
            jax.ShapeDtypeStruct((rows_send, 2 * width), bf16),
            jax.ShapeDtypeStruct((rows_part, 128), bf16),
        ],
        in_specs=[vmem] * 3 + [hbm] * 5 + [vmem] * 2,
        out_specs=[hbm] * 3 + [vmem] * 3,
        scratch_shapes=[
            pltpu.VMEM((tokens_dev, width), bf16),
            pltpu.VMEM((tokens_dev, width), bf16),
            pltpu.VMEM((tokens_dev, width), bf16),
            pltpu.VMEM((width, tokens_dev), bf16),
            pltpu.VMEM((tokens_dev, width), bf16),
            pltpu.VMEM((tokens_dev, width), bf16),
            pltpu.VMEM((rows_own, 2 * width), bf16),
            pltpu.VMEM((rows_side, 2 * width), bf16),
            pltpu.VMEM((rows_own, 2 * width), bf16),
            pltpu.VMEM((2, rows_side, 2 * width), bf16),
            pltpu.VMEM((rows_own, 2 * tile), f32),
            pltpu.VMEM((2, rows_side, 2 * tile), f32),
            pltpu.VMEM((2, 3, keys_all, 2 * tile), f32),
            pltpu.VMEM((keys_all, 2 * tile), f32),
            pltpu.VMEM((2 * tokens_dev // (2 * tile), 1, 2 * tile), f32),
            pltpu.VMEM((rows_own, 2 * width), f32),
            pltpu.VMEM((2, rows_side, 2 * width), f32),
            pltpu.SemaphoreType.DMA((14,)),
        ]
        + stage,
        compiler_params=pltpu.CompilerParams(vmem_limit_bytes=56 * MIB),
        name="attention",
    )(above, below, side, q, kv, g, tok_t, cot, wp, tissue)


def to_next(array, axis):
    count = lax.axis_size(axis)
    return lax.ppermute(array, axis, [(i, (i + 1) % count) for i in range(count)])


def to_last(array, axis):
    count = lax.axis_size(axis)
    return lax.ppermute(array, axis, [((i + 1) % count, i) for i in range(count)])


def sum_kernel(pieces, pieces_ref, copies_ref):
    rows = pieces_ref.shape[0] // pieces
    pair = 2 * rows
    total = jnp.zeros((pair, 128), f32)
    for i in range(pieces // 2):
        total = total + pieces_ref[i * pair : (i + 1) * pair].astype(f32)
    total = total[:rows] + total[rows:]
    total = jnp.concatenate([total, total], axis=0).astype(bf16)
    for i in range(pieces // 2):
        copies_ref[i * pair : (i + 1) * pair] = total


def summed_copies(pieces, count):
    return pl.pallas_call(
        functools.partial(sum_kernel, count),
        out_shape=jax.ShapeDtypeStruct(pieces.shape, bf16),
        compiler_params=pltpu.CompilerParams(vmem_limit_bytes=16 * MIB),
        name="summed_copies",
    )(pieces)


def total_over_devices(partial):
    axes = ("row", "col")
    count = lax.axis_size("row") * lax.axis_size("col")
    pieces = lax.all_to_all(partial.reshape(count, -1, 128), axes, 0, 0, tiled=True)
    copies = summed_copies(pieces.reshape(partial.shape), count).reshape(pieces.shape)
    return lax.all_to_all(copies, axes, 0, 0, tiled=True).reshape(partial.shape)


def unpack_kernel(scale, whole_ref, packed_ref, output_ref):
    width = output_ref.shape[0]
    for block in range((packed_ref.shape[1] + output_ref.shape[1]) // 128):
        value = whole_ref[block * width : (block + 1) * width].astype(f32) * scale
        column = block * 128
        if column < packed_ref.shape[1]:
            packed_ref[:, column : column + 128] = value
        else:
            column -= packed_ref.shape[1]
            output_ref[:, column : column + 128] = value


def unpack(whole, width, scale):
    return pl.pallas_call(
        functools.partial(unpack_kernel, scale),
        out_shape=[
            jax.ShapeDtypeStruct((width, 3 * width), f32),
            jax.ShapeDtypeStruct((width, width), f32),
        ],
        compiler_params=pltpu.CompilerParams(vmem_limit_bytes=24 * MIB),
        name="unpack",
    )(whole)


def per_device(tokens, tissue, cotangent, packed_weight, output_weight):
    rows_dev, cols_dev, width = tokens.shape
    ext_rows = rows_dev + 2 * RADIUS
    devices = lax.axis_size("row") * lax.axis_size("col")
    rows_part = -(-4 * width * (width // 128) // (8 * devices)) * 8 * devices
    total_scale = float(rows_dev * lax.axis_size("row") * cols_dev * lax.axis_size("col")) ** (-0.5)
    token_rows = tokens.reshape(-1, width)
    cotangent_rows = cotangent.reshape(-1, width)

    with_tissue = lambda a, b: jnp.concatenate([a, b.astype(bf16)[..., None]], axis=-1)
    above = to_next(with_tissue(tokens[-RADIUS:], tissue[-RADIUS:]), "row")
    below = to_last(with_tissue(tokens[:RADIUS], tissue[:RADIUS]), "row")
    left_cols = with_tissue(tokens[:, :RADIUS], tissue[:, :RADIUS])
    right_cols = with_tissue(tokens[:, -RADIUS:], tissue[:, -RADIUS:])
    left_cols = jnp.concatenate([above[:, :RADIUS], left_cols, below[:, :RADIUS]], axis=0)
    right_cols = jnp.concatenate([above[:, -RADIUS:], right_cols, below[:, -RADIUS:]], axis=0)
    from_left = to_next(right_cols, "col")
    from_right = to_last(left_cols, "col")
    pad = jnp.zeros((ext_rows, SIDE - 2 * RADIUS, width + 1), bf16)
    side = jnp.concatenate([from_right, from_left, pad], axis=1).reshape(-1, width + 1)

    q, kv, g, tok_t = project(token_rows, cotangent_rows, packed_weight, output_weight)
    attended, dq, dkv_own, to_left, to_right, partial = attention(
        above.reshape(-1, width + 1), below.reshape(-1, width + 1), side,
        q, kv, g, tok_t, cotangent_rows, packed_weight, tissue.T,
        (rows_dev * lax.axis_size("row"), cols_dev * lax.axis_size("col")), rows_part,
    )

    half = SIDE // 2

    def columns(sent):
        return sent[: ext_rows * half].reshape(ext_rows, half, 2 * width)[:, :RADIUS]

    from_right = columns(to_last(to_left, "col"))
    from_left = columns(to_next(to_right, "col"))
    dkv_own = dkv_own.reshape(ext_rows, cols_dev, 2 * width)
    first, last, inner = slice(None, RADIUS), slice(-RADIUS, None), slice(RADIUS, -RADIUS)

    def with_columns(rows):
        between = jnp.zeros((dkv_own[rows].shape[0], cols_dev - 2 * RADIUS, 2 * width), bf16)
        beside = jnp.concatenate([from_left[rows], between, from_right[rows]], axis=1)
        return dkv_own[rows].astype(f32) + beside.astype(f32)

    from_below = to_last(with_columns(first).astype(bf16), "row")
    from_above = to_next(with_columns(last).astype(bf16), "row")
    between = jnp.zeros((rows_dev - 2 * RADIUS, cols_dev, 2 * width), bf16)
    beside = jnp.concatenate([from_above, between, from_below], axis=0)
    dkv = with_columns(inner) + beside.astype(f32)
    dkv = dkv.astype(bf16).reshape(-1, 2 * width)

    contract = functools.partial(lax.dot_general, preferred_element_type=f32)
    layer_out = (
        token_rows.astype(f32) + jnp.dot(attended, output_weight, preferred_element_type=f32)
    ).astype(bf16)
    grad_tokens = (
        cotangent_rows.astype(f32)
        + contract(dq, packed_weight[:, :width], dims(1, 1))
        + contract(dkv, packed_weight[:, width:], dims(1, 1))
    ).astype(bf16)
    grad_packed, grad_output = unpack(total_over_devices(partial), width, total_scale)
    return (
        layer_out.reshape(rows_dev, cols_dev, width),
        grad_tokens.reshape(rows_dev, cols_dev, width),
        grad_packed,
        grad_output,
    )


def solution(mesh):
    in_specs = (P("row", "col", None), P("row", "col"), P("row", "col", None), P(), P())
    out_specs = (P("row", "col", None), P("row", "col", None), P(), P())
    return jax.shard_map(
        per_device, mesh=mesh, in_specs=in_specs, out_specs=out_specs, check_vma=False
    )
```

```python
import functools

import jax
import jax.numpy as jnp
from jax import lax
from jax.experimental import pallas as pl
from jax.experimental.pallas import tpu as pltpu
from jax.sharding import PartitionSpec as P

HEADS = 6
HEAD = 64
KERNEL = 7
RADIUS = 3
PAIR = 2 * HEAD
PAIRS = HEADS // 2
SIDE = 8
TILE_ROWS = 4
KEY_ROWS = TILE_ROWS + 2 * RADIUS
CHUNK = 48
SPAN = 4
PROJECT_STEPS = 2
FACTOR = HEAD ** (-0.5)
NEG = float("-inf")
MIB = 1024 * 1024
f32 = jnp.float32
bf16 = jnp.bfloat16


def dims(lhs, rhs):
    return (((lhs,), (rhs,)), ((), ()))


def project_kernel(
    tok_ref, cot_ref, wp_ref, wo_ref, q_ref, kv_ref, g_ref, tok_t_ref
):
    width = tok_ref.shape[1]
    tok = tok_ref[...]
    q = jnp.dot(tok, wp_ref[:, :width], preferred_element_type=f32).astype(bf16)
    q_ref[...] = (q * FACTOR).astype(bf16)
    kv_ref[...] = jnp.dot(tok, wp_ref[:, width:], preferred_element_type=f32).astype(bf16)
    g_ref[...] = lax.dot_general(
        cot_ref[...], wo_ref[...], dims(1, 1), preferred_element_type=f32
    ).astype(bf16)
    tok_t_ref[...] = tok.T


def project(tok, cot, wp, wo):
    count, width = tok.shape
    rows = count // PROJECT_STEPS
    block = lambda cols: pl.BlockSpec((rows, cols), lambda i: (i, 0))
    whole = lambda a: pl.BlockSpec(a.shape, lambda i: (0, 0))
    return pl.pallas_call(
        project_kernel,
        grid=(count // rows,),
        out_shape=[
            jax.ShapeDtypeStruct((count, width), bf16),
            jax.ShapeDtypeStruct((count, 2 * width), bf16),
            jax.ShapeDtypeStruct((count, width), bf16),
            jax.ShapeDtypeStruct((width, count), bf16),
        ],
        in_specs=[block(width), block(width), whole(wp), whole(wo)],
        out_specs=[
            block(width),
            block(2 * width),
            block(width),
            pl.BlockSpec((width, rows), lambda i: (0, i)),
        ],
        compiler_params=pltpu.CompilerParams(vmem_limit_bytes=56 * MIB),
        cost_estimate=pl.CostEstimate(
            flops=2 * count * width * 4 * width, bytes_accessed=14 * count * width, transcendentals=0
        ),
        name="project",
    )(tok, cot, wp, wo)


def attention_kernel(
    extents,
    above_ref, below_ref, side_ref, q_hbm, kv_hbm, g_hbm, tok_t_hbm, cot_hbm, wp_ref, tissue_ref,
    att_hbm, dq_hbm, dkv_own_hbm, to_left_ref, to_right_ref, part_ref,
    cot_ref, q_ref, g_ref, tok_t_ref, att_ref, dq_ref, dkv_own_ref, dkv_side_ref,
    kv_own_s, kv_aux_s, tis_own_s, tis_aux_s, win_s, self_s, gate_s, acc_own, acc_aux, sems, *stage,
):
    tokens_dev, width = q_ref.shape
    halo = above_ref.shape[0]
    rows_own = tokens_dev + 2 * halo
    rows_aux = side_ref.shape[0]
    cols = halo // RADIUS
    wide = cols // 2
    tile = TILE_ROWS * wide
    band = TILE_ROWS * cols
    bands = tokens_dev // band
    own_keys = KEY_ROWS * wide
    aux_keys = KEY_ROWS * SIDE
    keys_all = own_keys + aux_keys
    most = 4 * HEAD
    x_s, dp_s, top_s, pl_s, sg_s = (stage[2 * i : 2 * i + 2] for i in range(5))

    part = tokens_dev // 2
    early = []
    for i in range(2):
        rows = pl.ds(i * part, part)
        targets = (kv_own_s.at[pl.ds(halo + i * part, part)], q_ref.at[rows], g_ref.at[rows])
        for k, (source, target) in enumerate(zip((kv_hbm, q_hbm, g_hbm), targets)):
            early.append(pltpu.make_async_copy(source.at[rows], target, sems.at[3 * i + k]))
    for copy in early:
        copy.start()
    late = [
        pltpu.make_async_copy(tok_t_hbm, tok_t_ref, sems.at[6]),
        pltpu.make_async_copy(cot_hbm, cot_ref, sems.at[7]),
    ]
    done = tokens_dev // 2
    results = []
    for i in range(2):
        rows = pl.ds(i * done, done)
        ext = rows if i == 0 else pl.ds(done, rows_own - done)
        for k, (source, target, at) in enumerate(
            [
                (att_ref, att_hbm, rows),
                (dq_ref, dq_hbm, rows),
                (dkv_own_ref, dkv_own_hbm, ext),
            ]
        ):
            results.append(
                pltpu.make_async_copy(source.at[at], target.at[at], sems.at[8 + 3 * i + k])
            )

    def lanes(column):
        bias = jnp.where(column.astype(f32) > 0.5, 0.0, NEG)
        return jnp.broadcast_to(bias, (bias.shape[0], 2 * tile))

    def outer(rows_ref):
        return jnp.dot(
            rows_ref[:, :width], wp_ref[:, width:], preferred_element_type=f32
        ).astype(bf16)

    kv_own_s[:halo] = outer(above_ref)
    kv_own_s[halo + tokens_dev :] = outer(below_ref)
    kv_aux_s[0] = outer(side_ref)
    tis_own_s[:halo] = lanes(above_ref[:, width : width + 1])
    tis_own_s[halo + tokens_dev :] = lanes(below_ref[:, width : width + 1])
    tis_side = lanes(side_ref[:, width : width + 1])

    lane = lax.broadcasted_iota(jnp.int32, (1, 2 * tile), 1) % tile
    query_row = lane // wide
    query_col = lane % wide

    row_base = lax.axis_index("row") * (bands * TILE_ROWS)
    col_base = lax.axis_index("col") * cols

    def window(key, query, base, extent):
        start = jnp.clip(base + query - RADIUS, 0, extent - KERNEL) - base
        return jnp.where((key >= start) & (key < start + KERNEL), 0.0, NEG)

    own_col = lax.broadcasted_iota(jnp.int32, (wide, 2 * tile), 0)
    aux_place = lax.broadcasted_iota(jnp.int32, (SIDE, 2 * tile), 0)
    far = -(2**20)
    first_col = jnp.where(aux_place < RADIUS, aux_place + wide, aux_place - 2 * RADIUS)
    first_col = jnp.where(aux_place < 2 * RADIUS, first_col, far)
    second_col = jnp.where(aux_place < RADIUS, aux_place + cols, aux_place + wide - SIDE)
    second_col = jnp.where(
        (aux_place < RADIUS) | (aux_place >= SIDE - RADIUS), second_col, far
    )
    for half, aux_col in enumerate((first_col, second_col)):
        shift = half * wide
        own_in = window(own_col + shift, query_col + shift, col_base, extents[1])
        aux_in = window(aux_col, query_col + shift, col_base, extents[1])
        own_same = jnp.where(own_col == query_col, 0.0, NEG)
        for key_row in range(KEY_ROWS):
            own_rows = slice(key_row * wide, (key_row + 1) * wide)
            aux_rows = slice(own_keys + key_row * SIDE, own_keys + (key_row + 1) * SIDE)
            for kind, first in enumerate((0, 2 * TILE_ROWS, (bands - 1) * TILE_ROWS)):
                row_in = window(key_row - RADIUS, query_row, row_base + first, extents[0])
                win_s[half, kind, own_rows] = own_in + row_in
                win_s[half, kind, aux_rows] = aux_in + row_in
            if half == 0:
                row_same = jnp.where(query_row == key_row - RADIUS, 0.0, NEG)
                self_s[own_rows] = own_same + row_same
                self_s[aux_rows] = jnp.full((SIDE, 2 * tile), NEG, f32)
    tissue = tissue_ref[...].astype(f32).T
    for index in range(bands):
        row = jnp.concatenate(
            [tissue[index * TILE_ROWS + k : index * TILE_ROWS + k + 1] for k in range(TILE_ROWS)],
            axis=1,
        )
        across = jnp.broadcast_to(row, (2 * tile, band)).T
        tis_own_s[halo + index * band : halo + (index + 1) * band] = jnp.where(
            across > 0.5, 0.0, NEG
        )
        for half in range(2):
            pieces = [
                tissue[
                    index * TILE_ROWS + row : index * TILE_ROWS + row + 1,
                    half * wide : (half + 1) * wide,
                ]
                for row in range(TILE_ROWS)
            ]
            gate_s[2 * index + half] = jnp.concatenate(pieces * 2, axis=1)

    place = lax.broadcasted_iota(jnp.int32, (rows_aux, 1), 0) % SIDE

    def parts(array, begin, count):
        across = array.shape[1]
        return array.reshape(rows_own // cols, cols, across)[:, begin : begin + count].reshape(
            -1, across
        )

    def with_inner(own, side):
        first = parts(own, wide, SIDE)
        second = parts(own, wide - SIDE, SIDE)
        return (
            jnp.where(place < RADIUS, first, side),
            jnp.where(place >= SIDE - RADIUS, second, side),
        )

    early[0].wait()
    tis_aux_s[0], tis_aux_s[1] = with_inner(tis_own_s[...], tis_side)
    two_rows = lax.broadcasted_iota(jnp.int32, (2 * SIDE, 1), 0) % SIDE

    def fill(index, carry):
        rows = pl.ds(pl.multiple_of(index * 2 * SIDE, 2 * SIDE), 2 * SIDE)
        side = kv_aux_s[0, rows, :].astype(f32)

        def inner(first):
            at = [
                pl.ds(pl.multiple_of(index * 2 * cols, 2 * cols) + row * cols + first, 2 * SIDE)
                for row in range(2)
            ]
            return [kv_own_s[place, :].astype(f32) for place in at]

        one = jnp.concatenate([block[:SIDE] for block in inner(wide)], axis=0)
        two = jnp.concatenate([block[SIDE:] for block in inner(wide - 2 * SIDE)], axis=0)
        kv_aux_s[0, rows, :] = jnp.where(two_rows < RADIUS, one, side).astype(bf16)
        kv_aux_s[1, rows, :] = jnp.where(two_rows >= SIDE - RADIUS, two, side).astype(bf16)
        return carry

    row_pairs = rows_aux // (2 * SIDE)
    ready = (part // cols + RADIUS) // 2
    lax.fori_loop(0, ready, fill, 0, unroll=4)
    seen_rows = KEY_ROWS - TILE_ROWS
    acc_own[: seen_rows * cols] = jnp.zeros((seen_rows * cols, 2 * width), f32)
    acc_aux[:, : seen_rows * SIDE] = jnp.zeros((2, seen_rows * SIDE, 2 * width), f32)
    pl_s[1][...] = jnp.zeros((keys_all, HEADS * tile), bf16)
    sg_s[1][...] = jnp.zeros((keys_all, HEADS * tile), bf16)
    for copy in early[1:3]:
        copy.wait()
    for copy in late:
        copy.start()

    def split(block):
        head = lax.broadcasted_iota(jnp.int32, block.shape, 1) // HEAD
        zero = jnp.zeros_like(block)
        return jnp.concatenate(
            [jnp.where(head == i, block, zero) for i in range(block.shape[1] // HEAD)], axis=0
        )

    def corner(one, two):
        zero = jnp.zeros_like(one)
        return jnp.concatenate(
            [jnp.concatenate([one, zero], axis=1), jnp.concatenate([zero, two], axis=1)], axis=0
        )

    def own_at(index, half, row):
        return pl.ds(pl.multiple_of(index * band, band) + row * cols + half * wide, wide)

    def aux_at(index, begin, count):
        step = TILE_ROWS * SIDE
        return pl.ds(pl.multiple_of(index * step, step) + begin * SIDE, count * SIDE)

    def queries(ref, index, half):
        return jnp.concatenate([ref[own_at(index, half, row), :] for row in range(TILE_ROWS)], axis=0)

    def key_rows(index, half, at):
        rows = [kv_own_s[own_at(index, half, row), at] for row in range(KEY_ROWS)]
        return jnp.concatenate(rows + [kv_aux_s[half, aux_at(index, 0, KEY_ROWS), at]], axis=0)

    def score_stage(index, half):
        kind = jnp.where(index == 0, 0, jnp.where(index == bands - 1, 2, 1))
        tis_keys = jnp.concatenate(
            [tis_own_s[own_at(index, half, row)] for row in range(KEY_ROWS)]
            + [tis_aux_s[half, aux_at(index, 0, KEY_ROWS)]],
            axis=0,
        )
        bias = jnp.maximum(tis_keys, self_s[...]) + win_s[half, kind]
        q, g = queries(q_ref, index, half), queries(g_ref, index, half)
        keys = key_rows(index, half, slice(0, width))
        values = key_rows(index, half, slice(width, 2 * width))
        product = functools.partial(
            lax.dot_general, dimension_numbers=dims(1, 1), preferred_element_type=f32
        )
        rest = product(
            jnp.concatenate([keys[:, most:], values[:, most:]], axis=1),
            corner(split(q[:, most:]), split(g[:, most:])),
        )
        cut = HEADS * tile - 4 * tile
        scores = jnp.concatenate(
            [product(keys[:, :most], split(q[:, :most])), rest[:, :cut]], axis=1
        )
        scores = scores + jnp.concatenate([bias] * PAIRS, axis=1)
        x_s[half][...] = scores
        top_s[half][...] = jnp.max(scores, axis=0, keepdims=True)
        dp_s[half][:, : 4 * tile] = product(values[:, :most], split(g[:, :most]))
        dp_s[half][:, 4 * tile :] = rest[:, cut:]

    def softmax_stage(index, half):
        top = top_s[half][...]
        total = jnp.zeros((8, HEADS * tile), f32)
        inner = jnp.zeros((8, HEADS * tile), f32)
        fold = lambda a: jnp.sum(a.reshape(CHUNK // 8, 8, HEADS * tile), axis=0)
        for begin in range(0, keys_all, CHUNK):
            at = slice(begin, begin + CHUNK)
            terms = jnp.exp(x_s[half][at] - top)
            x_s[half][at] = terms
            total = total + fold(terms)
            inner = inner + fold(terms * dp_s[half][at])
        inverse = 1.0 / jnp.sum(total, axis=0, keepdims=True)
        delta = jnp.sum(inner, axis=0, keepdims=True) * inverse
        weight = inverse * jnp.concatenate([gate_s[2 * index + half]] * PAIRS, axis=1)
        for begin in range(0, keys_all, CHUNK):
            at = slice(begin, begin + CHUNK)
            probs = x_s[half][at] * weight
            pl_s[half][at] = probs.astype(bf16)
            sg_s[half][at] = (probs * (dp_s[half][at] - delta)).astype(bf16)

    def product_stage(index, half):
        keys = key_rows(index, half, slice(0, width))
        values = key_rows(index, half, slice(width, 2 * width))
        probs_low = pl_s[half][...]
        score_grad = sg_s[half][...]
        first_head = lax.broadcasted_iota(jnp.int32, (tile, PAIR), 1) < HEAD
        for pair in range(PAIRS):
            at = slice(pair * PAIR, (pair + 1) * PAIR)
            for rows, weight, scale, out_ref in (
                (values, probs_low, 1.0, att_ref),
                (keys, score_grad, FACTOR, dq_ref),
            ):
                both = lax.dot_general(
                    rows[:, at], weight[:, at], dims(0, 0), preferred_element_type=f32
                ).T
                mixed = (jnp.where(first_head, both[:tile], both[tile:]) * scale).astype(bf16)
                for row in range(TILE_ROWS):
                    out_ref[own_at(index, half, row), at] = mixed[row * wide : (row + 1) * wide]
        q, g = queries(q_ref, index, half), queries(g_ref, index, half)
        rest = jnp.dot(
            jnp.concatenate([probs_low[:, 4 * tile :], score_grad[:, 4 * tile :]], axis=1),
            corner(split(g[:, most:]), split(q[:, most:])),
            preferred_element_type=f32,
        )
        cut = width - most
        dk = jnp.dot(score_grad[:, : 4 * tile], split(q[:, :most]), preferred_element_type=f32)
        dv = jnp.dot(probs_low[:, : 4 * tile], split(g[:, :most]), preferred_element_type=f32)
        for grad, at in (
            (dk, slice(0, most)),
            (rest[:, cut:], slice(most, width)),
            (dv, slice(width, width + most)),
            (rest[:, :cut], slice(width + most, 2 * width)),
        ):
            for row in range(KEY_ROWS):
                piece = grad[row * wide : (row + 1) * wide]
                if row < seen_rows:
                    acc_own[own_at(index, half, row), at] += piece
                else:
                    acc_own[own_at(index, half, row), at] = piece
            seen = own_keys + seen_rows * SIDE
            acc_aux[half, aux_at(index, 0, seen_rows), at] += grad[own_keys:seen]
            acc_aux[half, aux_at(index, seen_rows, TILE_ROWS), at] = grad[seen:]

    def merge(index, carry):
        rows = pl.ds(pl.multiple_of(index * 2 * SIDE, 2 * SIDE), 2 * SIDE)
        one, two = acc_aux[0, rows, :], acc_aux[1, rows, :]
        dkv_side_ref[rows, :] = jnp.where(
            two_rows < RADIUS, two, jnp.where(two_rows < 2 * RADIUS, one, 0.0)
        ).astype(bf16)
        one = jnp.where(two_rows < RADIUS, one, 0.0)
        two = jnp.where(two_rows >= SIDE - RADIUS, two, 0.0)
        for row in range(2):
            start = pl.multiple_of(index * 2 * cols, 2 * cols) + row * cols
            at = slice(row * SIDE, (row + 1) * SIDE)
            own = acc_own[pl.ds(start, cols), :]
            own = jnp.concatenate(
                [
                    own[: wide - SIDE],
                    own[wide - SIDE : wide] + two[at],
                    own[wide : wide + SIDE] + one[at],
                    own[wide + SIDE :],
                ],
                axis=0,
            )
            dkv_own_ref[pl.ds(start, cols), :] = own.astype(bf16)
        return carry

    final = done // (2 * cols)
    more_keys = (part // cols - TILE_ROWS - RADIUS) // (TILE_ROWS * SPAN)
    first_done = bands // 2 // SPAN + 1
    score_stage(0, 0)

    def step(group, carry):
        @pl.when(group == more_keys)
        def _():
            for copy in early[3:]:
                copy.wait()
            lax.fori_loop(ready, row_pairs, fill, 0, unroll=4)

        @pl.when(group == first_done)
        def _():
            lax.fori_loop(0, final, merge, 0, unroll=4)
            for copy in results[:3]:
                copy.start()

        for slot in range(2 * SPAN):
            index = group * SPAN + slot // 2
            half = slot % 2
            if half == 0:
                product_stage(jnp.maximum(index - 1, 0), 1)
            else:
                product_stage(index, 0)
            softmax_stage(index, half)
            if half == 0:
                score_stage(index, 1)
            else:
                score_stage(jnp.minimum(index + 1, bands - 1), 0)
        return carry

    lax.fori_loop(0, bands // SPAN, step, 0)
    product_stage(bands - 1, 1)

    lax.fori_loop(final, row_pairs, merge, 0, unroll=4)
    for copy in results[3:]:
        copy.start()
    for copy in late:
        copy.wait()
    send_row = lax.broadcasted_iota(jnp.int32, (128, 256), 0)
    side_row = lax.broadcasted_iota(jnp.int32, (128, 256), 1)
    place = (send_row // (SIDE // 2)) * SIDE + send_row % (SIDE // 2)
    for begin, send_ref in ((RADIUS, to_left_ref), (0, to_right_ref)):
        pick = jnp.where(side_row == place + begin, 1.0, 0.0).astype(bf16)
        for first in range(0, send_ref.shape[0], 128):
            count = min(128, send_ref.shape[0] - first)
            source = dkv_side_ref[2 * first : min(2 * (first + count), dkv_side_ref.shape[0])]
            send_ref[first : first + count] = jnp.dot(
                pick[:count, : source.shape[0]], source, preferred_element_type=f32
            ).astype(bf16)
    outside = jnp.concatenate(
        [above_ref[:, :width], below_ref[:, :width], side_ref[:, :width]], axis=0
    )

    def put(block, value):
        value = value.astype(bf16)
        for i in range(value.shape[1] // 128):
            part_ref[(block + i) * width : (block + i + 1) * width] = value[
                :, i * 128 : (i + 1) * 128
            ]

    columns = width // 128
    put(0, jnp.dot(tok_t_ref[...], dq_ref[...], preferred_element_type=f32))
    for begin in range(0, 2 * width, 256):
        at = slice(begin, begin + 256)
        grad_outside = jnp.concatenate(
            [dkv_own_ref[:halo, at], dkv_own_ref[halo + tokens_dev :, at], dkv_side_ref[:, at]],
            axis=0,
        )
        put(
            columns + begin // 128,
            jnp.dot(
                tok_t_ref[...],
                dkv_own_ref[halo : halo + tokens_dev, at],
                preferred_element_type=f32,
            )
            + lax.dot_general(outside, grad_outside, dims(0, 0), preferred_element_type=f32),
        )
    put(3 * columns, lax.dot_general(
            att_ref[...], cot_ref[...], dims(0, 0), preferred_element_type=f32
        ))
    used = 4 * width * columns
    if used < part_ref.shape[0]:
        part_ref[used:] = jnp.zeros((part_ref.shape[0] - used, 128), bf16)
    for copy in results:
        copy.wait()


def attention(
    above, below, side, q, kv, g, tok_t, cot, wp, tissue, extents, rows_part
):
    tokens_dev, width = cot.shape
    rows_own = tokens_dev + 2 * above.shape[0]
    rows_side = side.shape[0]
    cols = tissue.shape[0]
    tile = TILE_ROWS * cols // 2
    keys_all = KEY_ROWS * (cols // 2 + SIDE)
    rows_send = -(-rows_side // 32) * 16
    vmem = pl.BlockSpec(memory_space=pltpu.VMEM)
    hbm = pl.BlockSpec(memory_space=pl.ANY)
    stage = []
    for shape, kind in (
        ((keys_all, HEADS * tile), f32),
        ((keys_all, HEADS * tile), f32),
        ((1, HEADS * tile), f32),
        ((keys_all, HEADS * tile), bf16),
        ((keys_all, HEADS * tile), bf16),
    ):
        stage += [pltpu.VMEM(shape, kind)] * 2
    return pl.pallas_call(
        functools.partial(attention_kernel, extents),
        out_shape=[
            jax.ShapeDtypeStruct((tokens_dev, width), bf16),
            jax.ShapeDtypeStruct((tokens_dev, width), bf16),
            jax.ShapeDtypeStruct((rows_own, 2 * width), bf16),
            jax.ShapeDtypeStruct((rows_send, 2 * width), bf16),
            jax.ShapeDtypeStruct((rows_send, 2 * width), bf16),
            jax.ShapeDtypeStruct((rows_part, 128), bf16),
        ],
        in_specs=[vmem] * 3 + [hbm] * 5 + [vmem] * 2,
        out_specs=[hbm] * 3 + [vmem] * 3,
        scratch_shapes=[
            pltpu.VMEM((tokens_dev, width), bf16),
            pltpu.VMEM((tokens_dev, width), bf16),
            pltpu.VMEM((tokens_dev, width), bf16),
            pltpu.VMEM((width, tokens_dev), bf16),
            pltpu.VMEM((tokens_dev, width), bf16),
            pltpu.VMEM((tokens_dev, width), bf16),
            pltpu.VMEM((rows_own, 2 * width), bf16),
            pltpu.VMEM((rows_side, 2 * width), bf16),
            pltpu.VMEM((rows_own, 2 * width), bf16),
            pltpu.VMEM((2, rows_side, 2 * width), bf16),
            pltpu.VMEM((rows_own, 2 * tile), f32),
            pltpu.VMEM((2, rows_side, 2 * tile), f32),
            pltpu.VMEM((2, 3, keys_all, 2 * tile), f32),
            pltpu.VMEM((keys_all, 2 * tile), f32),
            pltpu.VMEM((2 * tokens_dev // (2 * tile), 1, 2 * tile), f32),
            pltpu.VMEM((rows_own, 2 * width), f32),
            pltpu.VMEM((2, rows_side, 2 * width), f32),
            pltpu.SemaphoreType.DMA((14,)),
        ]
        + stage,
        compiler_params=pltpu.CompilerParams(vmem_limit_bytes=56 * MIB),
        name="attention",
    )(above, below, side, q, kv, g, tok_t, cot, wp, tissue)


def to_next(array, axis):
    count = lax.axis_size(axis)
    return lax.ppermute(array, axis, [(i, (i + 1) % count) for i in range(count)])


def to_last(array, axis):
    count = lax.axis_size(axis)
    return lax.ppermute(array, axis, [((i + 1) % count, i) for i in range(count)])


def sum_kernel(pieces, pieces_ref, copies_ref):
    rows = pieces_ref.shape[0] // pieces
    pair = 2 * rows
    total = jnp.zeros((pair, 128), f32)
    for i in range(pieces // 2):
        total = total + pieces_ref[i * pair : (i + 1) * pair].astype(f32)
    total = total[:rows] + total[rows:]
    total = jnp.concatenate([total, total], axis=0).astype(bf16)
    for i in range(pieces // 2):
        copies_ref[i * pair : (i + 1) * pair] = total


def summed_copies(pieces, count):
    return pl.pallas_call(
        functools.partial(sum_kernel, count),
        out_shape=jax.ShapeDtypeStruct(pieces.shape, bf16),
        compiler_params=pltpu.CompilerParams(vmem_limit_bytes=16 * MIB),
        name="summed_copies",
    )(pieces)


def total_over_devices(partial):
    axes = ("row", "col")
    count = lax.axis_size("row") * lax.axis_size("col")
    pieces = lax.all_to_all(partial.reshape(count, -1, 128), axes, 0, 0, tiled=True)
    copies = summed_copies(pieces.reshape(partial.shape), count).reshape(pieces.shape)
    return lax.all_to_all(copies, axes, 0, 0, tiled=True).reshape(partial.shape)


def unpack_kernel(scale, whole_ref, packed_ref, output_ref):
    width = output_ref.shape[0]

    def put(out_ref):
        for block in range(width // 128):
            value = whole_ref[block * width : (block + 1) * width].astype(f32) * scale
            out_ref[:, block * 128 : (block + 1) * 128] = value

    last = pl.program_id(0) == 3

    @pl.when(jnp.logical_not(last))
    def _():
        put(packed_ref)

    @pl.when(last)
    def _():
        put(output_ref)


def unpack(whole, width, scale):
    return pl.pallas_call(
        functools.partial(unpack_kernel, scale),
        grid=(4,),
        out_shape=[
            jax.ShapeDtypeStruct((width, 3 * width), f32),
            jax.ShapeDtypeStruct((width, width), f32),
        ],
        in_specs=[pl.BlockSpec((width * (width // 128), 128), lambda i: (i, 0))],
        out_specs=[
            pl.BlockSpec((width, width), lambda i: (0, jnp.minimum(i, 2))),
            pl.BlockSpec((width, width), lambda i: (0, 0)),
        ],
        compiler_params=pltpu.CompilerParams(vmem_limit_bytes=24 * MIB),
        name="unpack",
    )(whole)


def per_device(tokens, tissue, cotangent, packed_weight, output_weight):
    rows_dev, cols_dev, width = tokens.shape
    ext_rows = rows_dev + 2 * RADIUS
    devices = lax.axis_size("row") * lax.axis_size("col")
    rows_part = -(-4 * width * (width // 128) // (8 * devices)) * 8 * devices
    total_scale = float(rows_dev * lax.axis_size("row") * cols_dev * lax.axis_size("col")) ** (-0.5)
    token_rows = tokens.reshape(-1, width)
    cotangent_rows = cotangent.reshape(-1, width)

    with_tissue = lambda a, b: jnp.concatenate([a, b.astype(bf16)[..., None]], axis=-1)
    above = to_next(with_tissue(tokens[-RADIUS:], tissue[-RADIUS:]), "row")
    below = to_last(with_tissue(tokens[:RADIUS], tissue[:RADIUS]), "row")
    left_cols = with_tissue(tokens[:, :RADIUS], tissue[:, :RADIUS])
    right_cols = with_tissue(tokens[:, -RADIUS:], tissue[:, -RADIUS:])
    left_cols = jnp.concatenate([above[:, :RADIUS], left_cols, below[:, :RADIUS]], axis=0)
    right_cols = jnp.concatenate([above[:, -RADIUS:], right_cols, below[:, -RADIUS:]], axis=0)
    from_left = to_next(right_cols, "col")
    from_right = to_last(left_cols, "col")
    pad = jnp.zeros((ext_rows, SIDE - 2 * RADIUS, width + 1), bf16)
    side = jnp.concatenate([from_right, from_left, pad], axis=1).reshape(-1, width + 1)

    q, kv, g, tok_t = project(token_rows, cotangent_rows, packed_weight, output_weight)
    attended, dq, dkv_own, to_left, to_right, partial = attention(
        above.reshape(-1, width + 1), below.reshape(-1, width + 1), side,
        q, kv, g, tok_t, cotangent_rows, packed_weight, tissue.T,
        (rows_dev * lax.axis_size("row"), cols_dev * lax.axis_size("col")), rows_part,
    )

    half = SIDE // 2

    def columns(sent):
        return sent[: ext_rows * half].reshape(ext_rows, half, 2 * width)[:, :RADIUS]

    from_right = columns(to_last(to_left, "col"))
    from_left = columns(to_next(to_right, "col"))
    dkv_own = dkv_own.reshape(ext_rows, cols_dev, 2 * width)
    first, last, inner = slice(None, RADIUS), slice(-RADIUS, None), slice(RADIUS, -RADIUS)

    def with_columns(rows):
        between = jnp.zeros((dkv_own[rows].shape[0], cols_dev - 2 * RADIUS, 2 * width), bf16)
        beside = jnp.concatenate([from_left[rows], between, from_right[rows]], axis=1)
        return dkv_own[rows].astype(f32) + beside.astype(f32)

    from_below = to_last(with_columns(first).astype(bf16), "row")
    from_above = to_next(with_columns(last).astype(bf16), "row")
    between = jnp.zeros((rows_dev - 2 * RADIUS, cols_dev, 2 * width), bf16)
    beside = jnp.concatenate([from_above, between, from_below], axis=0)
    dkv = with_columns(inner) + beside.astype(f32)
    dkv = dkv.astype(bf16).reshape(-1, 2 * width)

    contract = functools.partial(lax.dot_general, preferred_element_type=f32)
    layer_out = (
        token_rows.astype(f32) + jnp.dot(attended, output_weight, preferred_element_type=f32)
    ).astype(bf16)
    grad_tokens = (
        cotangent_rows.astype(f32)
        + contract(dq, packed_weight[:, :width], dims(1, 1))
        + contract(dkv, packed_weight[:, width:], dims(1, 1))
    ).astype(bf16)
    grad_packed, grad_output = unpack(total_over_devices(partial), width, total_scale)
    return (
        layer_out.reshape(rows_dev, cols_dev, width),
        grad_tokens.reshape(rows_dev, cols_dev, width),
        grad_packed,
        grad_output,
    )


def solution(mesh):
    in_specs = (P("row", "col", None), P("row", "col"), P("row", "col", None), P(), P())
    out_specs = (P("row", "col", None), P("row", "col", None), P(), P())
    return jax.shard_map(
        per_device, mesh=mesh, in_specs=in_specs, out_specs=out_specs, check_vma=False
    )
```
